256 devices in a mesh: section: 8 (over y, core), tile: 32 (over x, z).
Axes of the slice: x: 4, y: 4, z: 8, core: 2. Of those that a mesh axis runs over, the one named last changes fastest.
Arguments:
- latent: bfloat16 [1, 18432, 1536], P(None, 'tile'), may hold values from -6 to 6
- w_qkv: bfloat16 [8, 1536, 4608], P('section', 'tile'), may hold values from -0.15625 to 0.15625
- mod_shift: float32 [8, 1536], P('section'), may hold values from -3 to 3
- mod_scale: float32 [8, 1536], P('section'), may hold values from 0.25 to 1.75
- attn_gate: float32 [8, 1536], P('section'), may hold values from 0.5 to 1.5
- qk_gain: float32 [8, 128], P('section'), may hold values from 0.8 to 2
- slot_tile: int32 [96], replicated, may hold values from 0 to 95, as said below
- window_tiles: int32 [96, 27], replicated, may hold values from -1 to 95, as said below
Outputs:
- layer_states: bfloat16 [8, 1, 18432, 1536], P('section', None, 'tile')
The draws below stay inside these ranges and needn't reach their ends.
Inputs may be any that keep to these rules, and one draw needn't show every extreme that they name: `slot_tile`: A permutation of the 96 tile ids. `window_tiles`: row t lists the tiles of the 3 x 3 x 3 tile window around tile t in the latent's frame, height and width (t itself included), -1 where the window leaves the latent; no id twice in a row. Every listed tile is stored in a slot of the same tile device as t's slot or of one of the two tile devices beside it, cyclically (device i holds slots i * 3 to (i + 1) * 3 - 1).
All inputs are finite; a program needn't handle non-finite values.
Results may differ from the reference program's by a relative error of at most 0.01.
Values may be sent and summed in bfloat16 or wider, within the bound.
A program may use at most 128 MiB of HBM per device.

```python
import math
import jax
import jax.numpy as jnp
from jax import lax

D = 1536
HEADS = 12
HEAD_DIM = 128
TILE = 192
GRID_H = 1
GRID_W = 3
NB = 27
MICRO = 1
NT = 96
SEQ = 18432
LAYERS = 8
N_TILE = 32


def layout_tables(key):
    per_device = GRID_H * GRID_W
    tiles_all = N_TILE * per_device
    label_key, rotate_key, mirror_key, scramble_key = jax.random.split(key, 4)
    labels = jax.random.permutation(label_key, tiles_all).astype(jnp.int32)
    rotation = jax.random.randint(rotate_key, (), 0, N_TILE).astype(jnp.int32)
    mirror = jax.random.randint(mirror_key, (), 0, 2).astype(jnp.int32)
    device_ids = jnp.arange(N_TILE, dtype=jnp.int32)
    frame_rows = jnp.where(mirror == 0, (device_ids - rotation) % N_TILE, (rotation - device_ids) % N_TILE)
    scramble = jax.vmap(lambda sub_key: jax.random.permutation(sub_key, per_device))(jax.random.split(scramble_key, N_TILE)).astype(jnp.int32)
    logical = frame_rows[:, None] * per_device + scramble
    slot_tiles = labels[logical.reshape(-1)]
    logical_ids = jnp.arange(tiles_all, dtype=jnp.int32)
    frame_ids = logical_ids // per_device
    row_ids = logical_ids % per_device // GRID_W
    col_ids = logical_ids % GRID_W
    entries = []
    for step_frame in (-1, 0, 1):
        for step_row in (-1, 0, 1):
            for step_col in (-1, 0, 1):
                near_frame = frame_ids + step_frame
                near_row = row_ids + step_row
                near_col = col_ids + step_col
                inside = (near_frame >= 0) & (near_frame < N_TILE) & (near_row >= 0) & (near_row < GRID_H)
                inside = inside & (near_col >= 0) & (near_col < GRID_W)
                target = jnp.clip(near_frame, 0, N_TILE - 1) * per_device + jnp.clip(near_row, 0, GRID_H - 1) * GRID_W + jnp.clip(near_col, 0, GRID_W - 1)
                entries.append(jnp.where(inside, labels[target], -1))
    window_logical = jnp.stack(entries, axis=1)
    inverse = jnp.zeros((tiles_all,), jnp.int32).at[labels].set(logical_ids)
    return (slot_tiles, window_logical[inverse].astype(jnp.int32))


def draw_slot_tile(key, part):
    tables = layout_tables(key)
    return tables[0]


def draw_window_tiles(key, part):
    tables = layout_tables(key)
    return tables[1]


def block_levels(stream_key, dims, shards, least, largest):
    level = 1.0
    for dim, parts in shards:
        steps = jax.random.uniform(jax.random.fold_in(jax.random.fold_in(stream_key, 6), dim), (parts,), jnp.float32, least / len(shards), largest / len(shards))
        level = level * jnp.repeat(jnp.exp(steps), dims[dim] // parts).reshape((-1,) + (1,) * (len(dims) - 1 - dim))
    return level


def normal_values(rng, dims, scale, bound, pieces=(), held_as=jnp.bfloat16):
    array = jax.random.normal(rng, dims, jnp.float32) * scale
    if len(pieces) > 0:
        array = block_levels(rng, dims, pieces, -0.22, 0.18) * array
    return jnp.clip(array, min=-bound, max=bound).astype(held_as)


def setup_inputs(seed: int = 0) -> dict:
    seeds = jax.random.split(jax.random.key(seed), 9)
    return {
        "latent": normal_values(seeds[0], (MICRO, SEQ, D), 1.0, 6.0, ((1, 32),)),
        "w_qkv": normal_values(seeds[1], (LAYERS, D, 3 * D), D ** -0.5, 0.15625, ((0, 8), (1, 32))),
        "mod_shift": normal_values(seeds[2], (LAYERS, D), 0.5, 3.0, ((0, 8),), jnp.float32),
        "mod_scale": jnp.clip(1.0 + 0.15 * jax.random.normal(seeds[3], (LAYERS, D), jnp.float32), 0.25, 1.75),
        "attn_gate": jnp.clip(0.5 + 1.0 * jax.random.uniform(seeds[4], (LAYERS, D), jnp.float32) ** block_levels(seeds[4], (LAYERS, D), ((0, 8),), -0.2, 0.2), 0.5, 1.5),
        "qk_gain": jnp.clip(jnp.exp(math.log(2.0) - 0.9162907 * jax.random.uniform(seeds[5], (LAYERS, HEAD_DIM), jnp.float32) ** block_levels(seeds[5], (LAYERS, HEAD_DIM), ((0, 8),), -0.2, 0.2)), 0.8, 2.0),
        "slot_tile": draw_slot_tile(jax.random.fold_in(seeds[8], 71), 0),
        "window_tiles": draw_window_tiles(jax.random.fold_in(seeds[8], 71), 0),
    }


EPS = 1e-06

def modulate(hidden, shifts, scales):
    numbers = hidden.astype(jnp.float32)
    average = lax.optimization_barrier(jnp.mean(numbers, axis=-1, keepdims=True))
    centred = numbers - average
    spread = lax.optimization_barrier(jnp.mean(centred * centred, axis=-1, keepdims=True))
    normed = centred * lax.rsqrt(spread + EPS)
    return (normed * scales + shifts).astype(jnp.bfloat16)

def head_norm(numbers, gain_values):
    square_mean = lax.optimization_barrier(jnp.mean(numbers * numbers, axis=-1, keepdims=True))
    return (numbers * lax.rsqrt(square_mean + EPS) * gain_values).astype(jnp.bfloat16)

def block_layer(hidden, weights, shifts, scales, gate_values, gain_values, key_slots, usable):
    modded = modulate(hidden, shifts, scales)
    projected = jnp.dot(modded, weights, preferred_element_type=jnp.float32)
    seq_len = projected.shape[0]
    shaped = projected.reshape(seq_len, 3, HEADS, HEAD_DIM)
    queries = head_norm(shaped[:, 0], gain_values).reshape(NT, TILE, HEADS, HEAD_DIM)
    key_heads = head_norm(shaped[:, 1], gain_values).reshape(NT, TILE, HEADS, HEAD_DIM)
    values = shaped[:, 2].astype(jnp.bfloat16).reshape(NT, TILE, HEADS, HEAD_DIM)

    def one_tile(tile_index):
        chosen = key_slots[tile_index]
        near_keys = key_heads[chosen].astype(jnp.float32).reshape(NB * TILE, HEADS, HEAD_DIM)
        near_values = values[chosen].astype(jnp.float32).reshape(NB * TILE, HEADS, HEAD_DIM)
        key_mask = jnp.repeat(usable[tile_index], TILE)
        scores = jnp.einsum('qhd,khd->hqk', queries[tile_index].astype(jnp.float32), near_keys) * HEAD_DIM ** (-0.5)
        scores = jnp.where(key_mask[None, None, :], scores, -jnp.inf)
        row_max = lax.optimization_barrier(jnp.max(scores, axis=-1, keepdims=True))
        powers = jnp.exp(scores - row_max)
        row_sum = lax.optimization_barrier(jnp.sum(powers, axis=-1, keepdims=True))
        probs = (powers / row_sum).astype(jnp.bfloat16)
        attended = jnp.einsum('hqk,khd->qhd', probs.astype(jnp.float32), near_values)
        return attended.reshape(TILE, D)
    attended = lax.map(one_tile, jnp.arange(NT, dtype=jnp.int32)).reshape(seq_len, D)
    return (hidden.astype(jnp.float32) + gate_values * attended).astype(jnp.bfloat16)

def reference(latent, w_qkv, mod_shift, mod_scale, attn_gate, qk_gain, slot_tile, window_tiles):
    slot_ids = jnp.arange(NT, dtype=jnp.int32)
    inverse = jnp.zeros((NT,), jnp.int32).at[slot_tile].set(slot_ids)
    listed = window_tiles[slot_tile]
    usable = listed >= 0
    key_slots = inverse[jnp.maximum(listed, 0)]
    collected = []
    for layer_index in range(LAYERS):
        collected.append([])
    for micro_index in range(MICRO):
        hidden = latent[micro_index]
        for layer_index in range(LAYERS):
            hidden = block_layer(hidden, w_qkv[layer_index], mod_shift[layer_index], mod_scale[layer_index], attn_gate[layer_index], qk_gain[layer_index], key_slots, usable)
            collected[layer_index].append(hidden)
    return jnp.stack([jnp.stack(layer_list) for layer_list in collected])
```

```python
import functools
import math

import jax
import jax.numpy as jnp
from jax import lax
from jax.experimental import pallas as pl
from jax.experimental.pallas import tpu as pltpu
from jax.sharding import PartitionSpec as P

MESH = pl.DeviceIdType.MESH
HEAD = 128
SLOTS = 3
NY = 4
NX = 4
EPS = 1e-06
NEG = -1e30


def kernel(
    layers, nx, nz, heads, tokens, lat, wp, par, bias, out,
    hbuf, mod, wbuf, parbuf, qbuf, kvo, kvn, acc,
    loc_sem, a2a_s, a2a_r, par_s, par_r, z_s, z_r, x_s, x_r, c_s, c_r, cp_s, cp_r,
    kv_s, kv_r, g_s, g_r, o_s, o_r, o_l,
):
    width = NY * heads * HEAD
    half = tokens // 2
    chunk = half // SLOTS
    shard = wp.shape[1]
    n_tile = nx * nz
    section = lax.axis_index("section")
    t = lax.axis_index("tile")
    y, c = section // 2, section % 2
    x, z = t // nz, t % nz
    sib = (2 * y + 1 - c, t)
    t_next = (section, (t + 1) % n_tile)
    t_prev = (section, (t + n_tile - 1) % n_tile)
    z_next = (section, x * nz + (z + 1) % nz)
    z_prev = (section, x * nz + (z + nz - 1) % nz)
    x_next = (section, ((x + 1) % nx) * nz + z)
    x_prev = (section, ((x + nx - 1) % nx) * nz + z)

    def y_peer(d):
        return (2 * ((y + d) % NY) + c, t)

    def remote(src, dst, send, recv, device):
        return pltpu.make_async_remote_copy(
            src_ref=src, dst_ref=dst, send_sem=send, recv_sem=recv, device_id=device, device_id_type=MESH
        )

    partners = [y_peer(1), y_peer(2), y_peer(3), sib, t_next, t_prev]
    if nz > 1:
        partners += [z_next, z_prev]
    if nx > 1:
        partners += [x_next, x_prev]
    load_h = pltpu.make_async_copy(lat.at[0, pl.ds(pl.multiple_of(half * c, 16), half)], hbuf.at[0], loc_sem.at[0])
    load_h.start()
    own_rows = pl.ds(pl.multiple_of(shard * t, 16), shard)
    load_w = pltpu.make_async_copy(wp.at[y], wbuf.at[section, own_rows], loc_sem.at[1])
    load_w.start()
    load_p = pltpu.make_async_copy(par, parbuf.at[section], loc_sem.at[2])
    load_p.start()
    barrier = pltpu.get_barrier_semaphore()
    for device in partners:
        pl.semaphore_signal(barrier, inc=1, device_id=device, device_id_type=MESH)
    pl.semaphore_wait(barrier, len(partners))

    a2a = []
    for d in (1, 2, 3):
        a2a.append(
            remote(wp.at[(y + d) % NY], wbuf.at[section, own_rows], a2a_s.at[d - 1], a2a_r.at[d - 1], y_peer(d))
        )
        a2a.append(remote(par, parbuf.at[section], par_s.at[d - 1], par_r.at[d - 1], y_peer(d)))
    for copy in a2a:
        copy.start()
    load_w.wait()
    load_p.wait()
    for copy in a2a:
        copy.wait()

    def rows_of(xx, zz):
        return pl.ds(pl.multiple_of((xx * nz + zz) * shard, 16), shard)

    right_steps = nz // 2
    left_steps = (nz - 1) // 2

    def z_copy(layer, step, way):
        k = layer // 2
        zz = (z + nz - step) % nz if way == 0 else (z + step) % nz
        ref = wbuf.at[layer, rows_of(x, zz)]
        return remote(ref, ref, z_s.at[k, step, way], z_r.at[k, step, way], z_next if way == 0 else z_prev)

    def z_event(layer, step):
        if step > 0:
            if step - 1 < right_steps:
                z_copy(layer, step - 1, 0).wait()
            if step - 1 < left_steps:
                z_copy(layer, step - 1, 1).wait()
        if step < right_steps:
            z_copy(layer, step, 0).start()
        if step < left_steps:
            z_copy(layer, step, 1).start()

    z_events = right_steps + 1

    def x_copy(layer, step, way):
        k = layer // 2
        if step == 0:
            ref = wbuf.at[layer, pl.ds(pl.multiple_of(x * nz * shard, 16), nz * shard)]
        else:
            piece = nz * shard // 2
            xx = (x + nx - 1) % nx if way == 0 else (x + 1) % nx
            ref = wbuf.at[layer, pl.ds(pl.multiple_of(xx * nz * shard + way * piece, 16), piece)]
        return remote(ref, ref, x_s.at[k, step, way], x_r.at[k, step, way], x_next if way == 0 else x_prev)

    def x_event(layer, step):
        if nx == 1:
            return
        if step > 0:
            x_copy(layer, step - 1, 0).wait()
            x_copy(layer, step - 1, 1).wait()
        if step < 2:
            x_copy(layer, step, 0).start()
            x_copy(layer, step, 1).start()

    def core_copies(layer):
        k = layer // 2
        return (
            remote(wbuf.at[layer], wbuf.at[layer], c_s.at[k], c_r.at[k], sib),
            remote(parbuf.at[layer], parbuf.at[layer], cp_s.at[k], cp_r.at[k], sib),
        )

    @pl.when(c == 0)
    def _():
        for step in range(z_events):
            z_event(0, step)
        for step in range(3):
            x_event(0, step)
        for copy in core_copies(0):
            copy.start()

    @pl.when(c == 1)
    def _():
        for step in range(z_events):
            z_event(1, step)
        x_event(1, 0)

    load_h.wait()

    ones = jnp.ones((tokens, HEAD), jnp.bfloat16)

    def dot(a, b):
        return jnp.dot(a, b, preferred_element_type=jnp.float32)

    def head_norm(numbers, gain):
        square_mean = jnp.mean(numbers * numbers, axis=-1, keepdims=True)
        return (numbers * lax.rsqrt(square_mean + EPS) * gain).astype(jnp.bfloat16)

    def one_block(j, keys, values, allowed):
        scores = lax.dot_general(
            qbuf[j], keys, (((1,), (1,)), ((), ())), preferred_element_type=jnp.float32
        )
        scores = scores.reshape(SLOTS, chunk, tokens) + allowed
        powers = jnp.exp2(scores).astype(jnp.bfloat16).reshape(half, tokens)
        return dot(powers, jnp.concatenate([values, ones], axis=1))

    def layer_step(layer, carry):
        p = layer % 2
        q = 1 - p
        gathers_z = jnp.logical_and(c == p, layer + 2 < layers)
        gathers_x = jnp.logical_and(c != p, layer + 1 < layers)

        def at_z(step):
            @pl.when(gathers_z)
            def _():
                z_event(layer + 2, step)
                if step == z_events - 1:
                    x_event(layer + 2, 0)

        def at_x(step):
            @pl.when(gathers_x)
            def _():
                x_event(layer + 1, step)
                if step == 2:
                    for copy in core_copies(layer + 1):
                        copy.start()

        z_plan = [[] for _ in range(5)]
        for step in range(z_events):
            z_plan[step if step < z_events - 1 else 4].append(step)

        def at(place):
            for step in z_plan[place]:
                at_z(step)
            if place == 1:
                at_x(1)
            if place == 3:
                at_x(2)

        @pl.when(c != p)
        def _():
            for copy in core_copies(layer):
                copy.wait_recv()

        at(0)
        shifts = parbuf[layer, 0:1, :]
        scales = parbuf[layer, 1:2, :]
        gain = parbuf[layer, 3:4, 0:HEAD]
        for i in range(SLOTS):
            rows = pl.ds(i * chunk, chunk)
            numbers = hbuf[p, rows, :].astype(jnp.float32)
            average = jnp.mean(numbers, axis=-1, keepdims=True)
            centred = numbers - average
            spread = jnp.mean(centred * centred, axis=-1, keepdims=True)
            mod[rows, :] = (centred * lax.rsqrt(spread + EPS) * scales + shifts).astype(jnp.bfloat16)

        def kv_copy(j, kind):
            if kind == 0:
                ref = kvo.at[p, j, c]
                dst, device = ref, sib
            elif kind == 1:
                ref, dst, device = kvo.at[p, j, c], kvn.at[p, j, c, 0], t_next
            elif kind == 2:
                ref, dst, device = kvo.at[p, j, c], kvn.at[p, j, c, 1], t_prev
            else:
                ref = kvn.at[p, j, c, kind - 3]
                dst, device = ref, sib
            return remote(ref, dst, kv_s.at[p, j, kind], kv_r.at[p, j, kind], device)

        for j in range(heads):
            projected = dot(mod[...], wbuf[layer, :, 2 * HEAD * j : 2 * HEAD * (j + 1)])
            kvo[p, j, c, :, 0:HEAD] = head_norm(projected[:, 0:HEAD], gain)
            kvo[p, j, c, :, HEAD : 2 * HEAD] = projected[:, HEAD:].astype(jnp.bfloat16)
            for kind in (1, 2, 0):
                kv_copy(j, kind).start()
        at(1)
        queries = dot(mod[...], wbuf[layer, :, 2 * HEAD * heads :])
        query_gain = gain * (math.log2(math.e) / math.sqrt(HEAD))
        for j in range(heads):
            qbuf[j] = head_norm(queries[:, HEAD * j : HEAD * (j + 1)], query_gain)

        @pl.when(section == layer - 1)
        def _():
            keep_own().wait()

        @pl.when(2 * y + 1 - c == layer - 1)
        def _():
            keep_other().wait_send()

        for j in range(heads):
            kv_copy(j, 0).wait_recv()
            block = kvo[p, j].reshape(tokens, 2 * HEAD)
            acc[j] = one_block(j, block[:, 0:HEAD], block[:, HEAD:], bias[0])
        at(2)

        def near(j, side):
            block = kvn[p, j, side].reshape(tokens, 2 * HEAD)
            return one_block(j, block[:, 0:HEAD], block[:, HEAD:], bias[1 + side])

        def pass_on(j):
            for kind in (1, 2):
                kv_copy(j, kind).wait_recv()
            for kind in (3, 4):
                kv_copy(j, kind).start()
            acc[j] += near(j, c)

        def g_copy(j, d, back):
            place = (y + NY - d) % NY if back else y
            columns = pl.ds(pl.multiple_of((place * heads + j) * HEAD, HEAD), HEAD)
            ref = hbuf.at[q, :, columns]
            return remote(ref, ref, g_s.at[p, j, d - 1], g_r.at[p, j, d - 1], y_peer(d))

        def finish(j):
            for kind in (3, 4):
                kv_copy(j, kind).wait_recv()
            total = acc[j] + near(j, 1 - c)
            columns = pl.ds(pl.multiple_of((y * heads + j) * HEAD, HEAD), HEAD)
            attended = total[:, 0:HEAD] / total[:, HEAD:]
            gates = parbuf[layer, 2:3, columns]
            numbers = hbuf[p, :, columns].astype(jnp.float32) + gates * attended
            hbuf[q, :, columns] = numbers.astype(jnp.bfloat16)
            for d in (1, 3, 2):
                g_copy(j, d, False).start()

        pass_on(0)
        for j in range(1, heads):
            pass_on(j)
            if j == heads - 1:
                at(3)
            finish(j - 1)
        finish(heads - 1)
        at(4)
        for j in range(heads):
            for kind in range(5):
                kv_copy(j, kind).wait_send()
        for j in range(heads):
            for d in (1, 3, 2):
                g_copy(j, d, False).wait_send()
                g_copy(j, d, True).wait_recv()

        @pl.when(c == p)
        def _():
            for copy in core_copies(layer):
                copy.wait_send()

        @pl.when(section == layer)
        def _():
            keep_own().start()

        @pl.when(2 * y + 1 - c == layer)
        def _():
            keep_other().start()

        return carry

    def out_rows(place):
        return out.at[0, 0, pl.ds(pl.multiple_of(half * place, 16), half)]

    def keep_own():
        return pltpu.make_async_copy(hbuf.at[1 - c], out_rows(c), o_l.at[0])

    def keep_other():
        return remote(hbuf.at[c], out_rows(c), o_s.at[0], o_r.at[0], sib)

    lax.fori_loop(0, layers, layer_step, 0)

    @pl.when(section == layers - 1)
    def _():
        keep_own().wait()

    @pl.when(2 * y + 1 - c == layers - 1)
    def _():
        keep_other().wait_send()

    remote(hbuf.at[c], out_rows(1 - c), o_s.at[0], o_r.at[0], sib).wait_recv()


def allowed_bias(slot_tile, window_tiles, core, tokens):
    tiles = slot_tile.shape[0]
    tile_place = lax.axis_index("tile")
    tile_len = tokens // SLOTS
    half = tokens // 2
    slots = (tile_place * SLOTS + jnp.arange(-SLOTS, 2 * SLOTS, dtype=jnp.int32) + tiles) % tiles
    ids = jnp.sum(jnp.where(slots[:, None] == jnp.arange(tiles, dtype=jnp.int32)[None], slot_tile[None], 0), axis=1)
    own = ids[SLOTS : 2 * SLOTS]
    picked = own[:, None] == jnp.arange(tiles, dtype=jnp.int32)[None]
    listed = jnp.sum(jnp.where(picked[:, :, None], window_tiles[None], 0), axis=1)
    allowed = jnp.any(listed[:, :, None] == ids[None, None], axis=1)
    bias = jnp.where(allowed, 0.0, NEG).astype(jnp.float32)
    first, second = bias[jnp.array([0, 0, 1])], bias[jnp.array([1, 2, 2])]
    rows = jnp.where(core == 0, first, second)
    rows = jnp.repeat(rows.reshape(SLOTS, 3, SLOTS), tile_len, axis=2)
    blocks = [rows[:, 1]]
    for side in range(2):
        part = rows[:, :, side * half : (side + 1) * half]
        blocks.append(jnp.concatenate([part[:, 0], part[:, 2]], axis=1))
    return jnp.stack(blocks)[:, :, None, :]


def on_device(nx, latent, w_qkv, mod_shift, mod_scale, attn_gate, qk_gain, slot_tile, window_tiles):
    layers = lax.axis_size("section")
    n_tile = lax.axis_size("tile")
    nz = n_tile // nx
    _, tokens, width = latent.shape
    heads = width // HEAD // NY
    shard = w_qkv.shape[1]
    half = tokens // 2
    cols = 3 * heads * HEAD
    parts = w_qkv[0].reshape(shard, 3, NY, heads, HEAD)
    key_value = jnp.transpose(parts[:, 1:], (2, 0, 3, 1, 4)).reshape(NY, shard, 2 * heads * HEAD)
    query = jnp.transpose(parts[:, 0], (1, 0, 2, 3)).reshape(NY, shard, heads * HEAD)
    wp = jnp.concatenate([key_value, query], axis=-1)
    gain_row = jnp.pad(qk_gain, ((0, 0), (0, width - HEAD)))
    par = jnp.concatenate([mod_shift, mod_scale, attn_gate, gain_row, jnp.zeros((4, width), jnp.float32)], axis=0)
    bias = allowed_bias(slot_tile, window_tiles, lax.axis_index("section") % 2, tokens)
    pairs = layers // 2
    bf16, f32 = jnp.bfloat16, jnp.float32
    dma = pltpu.SemaphoreType.DMA
    any_space = pl.BlockSpec(memory_space=pl.ANY)
    return pl.pallas_call(
        functools.partial(kernel, layers, nx, nz, heads, tokens),
        out_shape=jax.ShapeDtypeStruct((1, 1, tokens, width), bf16),
        in_specs=[any_space, any_space, any_space, pl.BlockSpec(memory_space=pltpu.VMEM)],
        out_specs=any_space,
        scratch_shapes=[
            pltpu.VMEM((2, half, width), bf16),
            pltpu.VMEM((half, width), bf16),
            pltpu.VMEM((layers, width, cols), bf16),
            pltpu.VMEM((layers, 8, width), f32),
            pltpu.VMEM((heads, half, HEAD), bf16),
            pltpu.VMEM((2, heads, 2, half, 2 * HEAD), bf16),
            pltpu.VMEM((2, heads, 2, 2, half, 2 * HEAD), bf16),
            pltpu.VMEM((heads, half, 2 * HEAD), f32),
            dma((3,)), dma((3,)), dma((3,)), dma((3,)), dma((3,)),
            dma((pairs, 4, 2)), dma((pairs, 4, 2)), dma((pairs, 2, 2)), dma((pairs, 2, 2)),
            dma((pairs,)), dma((pairs,)), dma((pairs,)), dma((pairs,)),
            dma((2, heads, 5)), dma((2, heads, 5)), dma((2, heads, 3)), dma((2, heads, 3)),
            dma((1,)), dma((1,)), dma((1,)),
        ],
        compiler_params=pltpu.CompilerParams(
            collective_id=0, has_side_effects=True, vmem_limit_bytes=58 * 1024 * 1024
        ),
    )(latent, wp, par, bias)


def solution(mesh, nx=NX):
    return jax.shard_map(
        functools.partial(on_device, nx),
        mesh=mesh,
        in_specs=(
            P(None, "tile", None),
            P("section", "tile", None),
            P("section", None),
            P("section", None),
            P("section", None),
            P("section", None),
            P(),
            P(),
        ),
        out_specs=P("section", None, "tile", None),
        check_vma=False,
    )
```

```python
import functools
import math

import jax
import jax.numpy as jnp
from jax import lax
from jax.experimental import pallas as pl
from jax.experimental.pallas import tpu as pltpu
from jax.sharding import PartitionSpec as P

MESH = pl.DeviceIdType.MESH
HEAD = 128
SLOTS = 3
NY = 4
NX = 4
EPS = 1e-06
NEG = -1e30


def kernel(
    layers, nx, nz, heads, tokens, lat, w_part, shift_row, scale_row, gate_row, gain_row, slot_ids, windows, out,
    hbuf, mod, wbuf, parbuf, qbuf, kvo, kvn, acc, bias,
    loc_sem, a2a_s, a2a_r, par_s, par_r, z_s, z_r, x0_s, x0_r, x_s, x_r, xf_s, xf_r, c_s, c_r, cp_s, cp_r,
    kv_s, kv_r, g_s, g_r, o_s, o_r, o_l,
):
    width = NY * heads * HEAD
    half = tokens // 2
    chunk = half // SLOTS
    shard = w_part.shape[1]
    group = heads * HEAD
    n_tile = nx * nz
    section = lax.axis_index("section")
    t = lax.axis_index("tile")
    y, c = section // 2, section % 2
    x, z = t // nz, t % nz
    sib = (2 * y + 1 - c, t)
    t_next = (section, (t + 1) % n_tile)
    t_prev = (section, (t + n_tile - 1) % n_tile)
    z_next = (section, x * nz + (z + 1) % nz)
    z_prev = (section, x * nz + (z + nz - 1) % nz)
    x_next = (section, ((x + 1) % nx) * nz + z)
    x_prev = (section, ((x + nx - 1) % nx) * nz + z)

    def y_peer(d):
        return (2 * ((y + d) % NY) + c, t)

    def remote(src, dst, send, recv, device):
        return pltpu.make_async_remote_copy(
            src_ref=src, dst_ref=dst, send_sem=send, recv_sem=recv, device_id=device, device_id_type=MESH
        )

    partners = [y_peer(1), y_peer(2), y_peer(3), sib, t_next, t_prev]
    if nz > 1:
        partners += [z_next, z_prev]
    if nx > 1:
        partners += [x_next, x_prev, (section, ((x + 2) % nx) * nz + z)]
    load_h = pltpu.make_async_copy(lat.at[0, pl.ds(pl.multiple_of(half * c, 16), half)], hbuf.at[0], loc_sem.at[0])
    load_h.start()
    own_rows = pl.ds(pl.multiple_of(shard * t, 16), shard)

    def w_slices(place):
        for i in range(3):
            start = pl.multiple_of(i * width + place * group, HEAD)
            yield w_part.at[0, :, pl.ds(start, group)], wbuf.at[section, own_rows, i * group : (i + 1) * group]

    own_shard = wbuf.at[section, own_rows]
    for src, dst in w_slices(y):
        pltpu.make_async_copy(src, dst, loc_sem.at[1]).start()
    parbuf[section] = jnp.zeros(parbuf.shape[1:], jnp.float32)
    for i, row in enumerate((shift_row, scale_row, gate_row)):
        parbuf[section, i : i + 1, :] = row[...]
    parbuf[section, 3:4, 0:HEAD] = gain_row[...]
    barrier = pltpu.get_barrier_semaphore()
    for device in partners:
        pl.semaphore_signal(barrier, inc=1, device_id=device, device_id_type=MESH)
    pl.semaphore_wait(barrier, len(partners))

    def a2a_start():
        for d in (1, 3, 2):
            for src, dst in w_slices((y + d) % NY):
                remote(src, dst, a2a_s.at[d - 1], a2a_r.at[d - 1], y_peer(d)).start()
            remote(parbuf.at[section], parbuf.at[section], par_s.at[d - 1], par_r.at[d - 1], y_peer(d)).start()

    def a2a_whole(d):
        return (
            remote(own_shard, own_shard, a2a_s.at[d - 1], a2a_r.at[d - 1], sib),
            remote(parbuf.at[section], parbuf.at[section], par_s.at[d - 1], par_r.at[d - 1], sib),
        )

    @pl.when(y == 0)
    def _():
        a2a_start()

    @pl.when(y != 0)
    def _():
        for copy in a2a_whole(y):
            copy.wait_recv()
        a2a_start()

    pltpu.make_async_copy(own_shard, own_shard, loc_sem.at[1]).wait()

    def a2a_finish():
        for d in (1, 2, 3):
            for copy in a2a_whole(d):
                copy.wait_send()

            @pl.when(d != y)
            def _():
                for copy in a2a_whole(d):
                    copy.wait_recv()

    def rows_of(xx, zz):
        return pl.ds(pl.multiple_of((xx * nz + zz) * shard, 16), shard)

    right_steps = nz // 2
    left_steps = (nz - 1) // 2

    def z_copy(layer, step, way):
        k = layer // 2
        zz = (z + nz - step) % nz if way == 0 else (z + step) % nz
        ref = wbuf.at[layer, rows_of(x, zz)]
        return remote(ref, ref, z_s.at[k, step, way], z_r.at[k, step, way], z_next if way == 0 else z_prev)

    def z_event(layer, step):
        if step > 0:
            if step - 1 < right_steps:
                z_copy(layer, step - 1, 0).wait()
            if step - 1 < left_steps:
                z_copy(layer, step - 1, 1).wait()
        if step < right_steps:
            z_copy(layer, step, 0).start()
        if step < left_steps:
            z_copy(layer, step, 1).start()

    z_events = right_steps + 1

    block = nz * shard

    def x_rows(place, piece=None):
        if piece is None:
            return pl.ds(pl.multiple_of(place * block, 16), block)
        return pl.ds(pl.multiple_of(place * block + piece * (block // 2), 16), block // 2)

    def x_copy(layer, way, order):
        ref = wbuf.at[layer, x_rows(x, order if way == 0 else 1 - order)]
        k = layer // 2
        return remote(ref, ref, x_s.at[k, way, order], x_r.at[k, way, order], x_next if way == 0 else x_prev)

    def x_forward(layer, way):
        place = (x + nx - 1) % nx if way == 0 else (x + 1) % nx
        ref = wbuf.at[layer, x_rows(place, way)]
        k = layer // 2
        return remote(ref, ref, xf_s.at[k, way], xf_r.at[k, way], x_next if way == 0 else x_prev)

    def core_copy(layer, d):
        k = layer // 2
        ref = wbuf.at[layer, x_rows((x + d) % nx)]
        return remote(ref, ref, c_s.at[k, d], c_r.at[k, d], sib)

    def core_par(layer):
        k = layer // 2
        return remote(parbuf.at[layer], parbuf.at[layer], cp_s.at[k], cp_r.at[k], sib)

    def x_event(layer, step):
        if step == 0:
            core_copy(layer, 0).start()
            core_par(layer).start()
        if nx == 1:
            return
        if step == 0:
            for order in range(2):
                for way in range(2):
                    x_copy(layer, way, order).start()
        elif step == 1:
            for way in range(2):
                x_copy(layer, way, 0).wait_recv()
                x_forward(layer, way).start()
        else:
            for way in range(2):
                x_copy(layer, way, 1).wait_recv()
                core_copy(layer, nx - 1 if way == 0 else 1).start()
            for way in range(2):
                x_forward(layer, way).wait_recv()
            core_copy(layer, 2).start()
            for way in range(2):
                x_copy(layer, way, 0).wait_send()
                x_copy(layer, way, 1).wait_send()
                x_forward(layer, way).wait_send()

    def x_direct(shards):
        for zz in shards:
            ref = wbuf.at[0, rows_of(x, zz % nz)]
            for d in (1, 3, 2) if nx == 4 else ():
                to = (section, ((x + d) % nx) * nz + z)
                remote(ref, ref, x0_s.at[d - 1], x0_r.at[d - 1], to).start()

    def x_direct_whole(d, back):
        ref = wbuf.at[0, x_rows((x + nx - d) % nx if back else x)]
        return remote(ref, ref, x0_s.at[d - 1], x0_r.at[d - 1], sib)

    @pl.when(c == 0)
    def _():
        x_direct([z])
        for step in range(z_events):
            z_event(0, step)
            if step > 0:
                fresh = []
                if step - 1 < right_steps:
                    fresh.append(z + nz - step)
                if step - 1 < left_steps:
                    fresh.append(z + step)
                x_direct(fresh)
        core_copy(0, 0).start()
        core_par(0).start()
        a2a_finish()
        z_event(2, 0)
        if nx > 1:
            for d in (1, 3, 2):
                x_direct_whole(d, True).wait_recv()
                core_copy(0, nx - d).start()
                if d == 3:
                    z_event(2, 1)
            for d in (1, 3, 2):
                x_direct_whole(d, False).wait_send()
        else:
            z_event(2, 1)
        if z_events > 2:
            z_event(2, 2)

    @pl.when(c == 1)
    def _():
        a2a_finish()
        core_copy(0, 0).wait_recv()
        core_par(0).wait_recv()
        for step in range(z_events):
            z_event(1, step)
        for d in range(1, nx):
            core_copy(0, d).wait_recv()
        x_event(1, 0)

    tile_len = tokens // SLOTS
    n_slots = n_tile * SLOTS
    lanes = lax.broadcasted_iota(jnp.int32, (1, tokens), 1)

    def penalty(query_slot, frame, key_slot):
        place = (t + n_tile + frame) % n_tile
        key_id = slot_ids[place * SLOTS + key_slot]
        row = windows[pl.ds(slot_ids[t * SLOTS + query_slot], 1), :]
        listed = jnp.max(jnp.where(row == key_id, 1.0, 0.0), axis=1, keepdims=True)
        return jnp.where(listed > 0.0, 0.0, NEG)

    for i in range(SLOTS):
        query_slot = (half * c + chunk * i) // tile_len
        table = [[penalty(query_slot, frame, k) for k in range(SLOTS)] for frame in (-1, 0, 1)]

        def spread_over(tokens_at, pens):
            return jnp.where(tokens_at < tile_len, pens[0], jnp.where(tokens_at < 2 * tile_len, pens[1], pens[2]))

        bias[0, i] = spread_over(lanes, table[1])
        for side in range(2):
            low = spread_over(lanes + side * half, table[0])
            high = spread_over(lanes - half + side * half, table[2])
            bias[1 + side, i] = jnp.where(lanes < half, low, high)

    load_h.wait()

    ones = jnp.ones((tokens, HEAD), jnp.bfloat16)

    def dot(a, b):
        return jnp.dot(a, b, preferred_element_type=jnp.float32)

    def head_norm(numbers, gain):
        square_mean = jnp.mean(numbers * numbers, axis=-1, keepdims=True)
        return (numbers * lax.rsqrt(square_mean + EPS) * gain).astype(jnp.bfloat16)

    def one_block(j, keys, values, allowed):
        scores = lax.dot_general(
            qbuf[j], keys, (((1,), (1,)), ((), ())), preferred_element_type=jnp.float32
        )
        scores = scores.reshape(SLOTS, chunk, tokens) + allowed
        powers = jnp.exp2(scores).astype(jnp.bfloat16).reshape(half, tokens)
        return dot(powers, jnp.concatenate([values, ones], axis=1))

    def layer_step(layer, carry):
        p = layer % 2
        q = 1 - p

        def event(ahead, condition, do):
            ours = jnp.logical_and((layer + ahead) % 2 == c, layer + ahead < layers)
            if condition is not None:
                ours = jnp.logical_and(ours, condition)

            @pl.when(ours)
            def _():
                do(layer + ahead)

        def z_at(ahead, step):
            if step < z_events:
                event(ahead, None, lambda target: z_event(target, step))

        def at(place):
            if place == 0:
                z_at(2, 3)
                event(1, layer > 0, lambda target: x_event(target, 1))
                z_at(3, 0)
            elif place == 1:
                z_at(2, 4)
                event(2, None, lambda target: x_event(target, 0))
                event(1, layer > 0, lambda target: x_event(target, 2))
                event(1, layer == 0, lambda target: x_event(target, 1))
                z_at(3, 1)
            else:
                event(1, layer == 0, lambda target: x_event(target, 2))
                z_at(3, 2)

        @pl.when(jnp.logical_and(c != p, layer > 0))
        def _():
            core_par(layer).wait_recv()
            for d in range(nx):
                core_copy(layer, d).wait_recv()

        shifts = parbuf[layer, 0:1, :]
        scales = parbuf[layer, 1:2, :]
        gain = parbuf[layer, 3:4, 0:HEAD]
        for i in range(SLOTS):
            rows = pl.ds(i * chunk, chunk)
            numbers = hbuf[p, rows, :].astype(jnp.float32)
            average = jnp.mean(numbers, axis=-1, keepdims=True)
            centred = numbers - average
            spread = jnp.mean(centred * centred, axis=-1, keepdims=True)
            mod[rows, :] = (centred * lax.rsqrt(spread + EPS) * scales + shifts).astype(jnp.bfloat16)

        def kv_copy(j, kind):
            if kind == 0:
                ref = kvo.at[p, j, c]
                dst, device = ref, sib
            elif kind == 1:
                ref, dst, device = kvo.at[p, j, c], kvn.at[p, j, c, 0], t_next
            elif kind == 2:
                ref, dst, device = kvo.at[p, j, c], kvn.at[p, j, c, 1], t_prev
            else:
                ref = kvn.at[p, j, c, kind - 3]
                dst, device = ref, sib
            return remote(ref, dst, kv_s.at[p, j, kind], kv_r.at[p, j, kind], device)

        for j in range(heads):
            weights = jnp.concatenate(
                [wbuf[layer, :, i * group + HEAD * j : i * group + HEAD * (j + 1)] for i in (1, 2)], axis=1
            )
            projected = dot(mod[...], weights)
            kvo[p, j, c, :, 0:HEAD] = head_norm(projected[:, 0:HEAD], gain)
            kvo[p, j, c, :, HEAD : 2 * HEAD] = projected[:, HEAD:].astype(jnp.bfloat16)
            for kind in (1, 2, 0):
                kv_copy(j, kind).start()
            if j == 0:
                at(0)
        queries = dot(mod[...], wbuf[layer, :, 0:group])
        query_gain = gain * (math.log2(math.e) / math.sqrt(HEAD))
        for j in range(heads):
            qbuf[j] = head_norm(queries[:, HEAD * j : HEAD * (j + 1)], query_gain)

        @pl.when(section == layer - 1)
        def _():
            keep_own().wait()

        @pl.when(2 * y + 1 - c == layer - 1)
        def _():
            keep_other().wait_send()

        for j in range(heads):
            kv_copy(j, 0).wait_recv()
            block = kvo[p, j].reshape(tokens, 2 * HEAD)
            acc[j] = one_block(j, block[:, 0:HEAD], block[:, HEAD:], bias[0])

        def near(j, side):
            block = kvn[p, j, side].reshape(tokens, 2 * HEAD)
            return one_block(j, block[:, 0:HEAD], block[:, HEAD:], bias[1 + side])

        def pass_on(j):
            for kind in (1, 2):
                kv_copy(j, kind).wait_recv()
                kv_copy(j, kind + 2).start()
            acc[j] += near(j, c)

        def g_copy(j, d, back):
            place = (y + NY - d) % NY if back else y
            columns = pl.ds(pl.multiple_of((place * heads + j) * HEAD, HEAD), HEAD)
            ref = hbuf.at[q, :, columns]
            return remote(ref, ref, g_s.at[p, j, d - 1], g_r.at[p, j, d - 1], y_peer(d))

        def sends_to(d):
            return jnp.logical_or(layer < layers - 1, (y + d) % NY == NY - 1)

        def finish(j):
            for kind in (3, 4):
                kv_copy(j, kind).wait_recv()
            total = acc[j] + near(j, 1 - c)
            columns = pl.ds(pl.multiple_of((y * heads + j) * HEAD, HEAD), HEAD)
            attended = total[:, 0:HEAD] / total[:, HEAD:]
            gates = parbuf[layer, 2:3, columns]
            numbers = hbuf[p, :, columns].astype(jnp.float32) + gates * attended
            hbuf[q, :, columns] = numbers.astype(jnp.bfloat16)
            for d in (1, 3, 2):

                @pl.when(sends_to(d))
                def _():
                    g_copy(j, d, False).start()

        for j in range(heads):
            pass_on(j)
            finish(j)
            if j == 0:
                at(1)
        at(2)
        for j in range(heads):
            for kind in range(5):
                kv_copy(j, kind).wait_send()
        for d in (1, 3, 2):

            @pl.when(sends_to(d))
            def _():
                for j in range(heads):
                    g_copy(j, d, False).wait_send()

        @pl.when(sends_to(0))
        def _():
            for j in range(heads):
                for d in (1, 3, 2):
                    g_copy(j, d, True).wait_recv()

        @pl.when(c == p)
        def _():
            core_par(layer).wait_send()
            for d in range(nx):
                core_copy(layer, d).wait_send()

        @pl.when(section == layer)
        def _():
            keep_own().start()

        @pl.when(2 * y + 1 - c == layer)
        def _():
            keep_other().start()

        return carry

    def out_rows(place):
        return out.at[0, 0, pl.ds(pl.multiple_of(half * place, 16), half)]

    def keep_own():
        return pltpu.make_async_copy(hbuf.at[1 - c], out_rows(c), o_l.at[0])

    def keep_other():
        return remote(hbuf.at[c], out_rows(c), o_s.at[0], o_r.at[0], sib)

    lax.fori_loop(0, layers, layer_step, 0)

    @pl.when(section == layers - 1)
    def _():
        keep_own().wait()

    @pl.when(2 * y + 1 - c == layers - 1)
    def _():
        keep_other().wait_send()

    remote(hbuf.at[c], out_rows(1 - c), o_s.at[0], o_r.at[0], sib).wait_recv()


def on_device(nx, latent, w_qkv, mod_shift, mod_scale, attn_gate, qk_gain, slot_tile, window_tiles):
    layers = lax.axis_size("section")
    n_tile = lax.axis_size("tile")
    nz = n_tile // nx
    _, tokens, width = latent.shape
    heads = width // HEAD // NY
    shard = w_qkv.shape[1]
    half = tokens // 2
    cols = 3 * heads * HEAD
    pairs = layers // 2
    bf16, f32 = jnp.bfloat16, jnp.float32
    dma = pltpu.SemaphoreType.DMA
    any_space = pl.BlockSpec(memory_space=pl.ANY)
    in_vmem = pl.BlockSpec(memory_space=pltpu.VMEM)
    return pl.pallas_call(
        functools.partial(kernel, layers, nx, nz, heads, tokens),
        out_shape=jax.ShapeDtypeStruct((1, 1, tokens, width), bf16),
        in_specs=[any_space, any_space] + [in_vmem] * 4 + [pl.BlockSpec(memory_space=pltpu.SMEM), in_vmem],
        out_specs=any_space,
        scratch_shapes=[
            pltpu.VMEM((2, half, width), bf16),
            pltpu.VMEM((half, width), bf16),
            pltpu.VMEM((layers, width, cols), bf16),
            pltpu.VMEM((layers, 8, width), f32),
            pltpu.VMEM((heads, half, HEAD), bf16),
            pltpu.VMEM((2, heads, 2, half, 2 * HEAD), bf16),
            pltpu.VMEM((2, heads, 2, 2, half, 2 * HEAD), bf16),
            pltpu.VMEM((heads, half, 2 * HEAD), f32),
            pltpu.VMEM((3, SLOTS, 1, tokens), f32),
            dma((3,)), dma((3,)), dma((3,)), dma((3,)), dma((3,)),
            dma((pairs, 4, 2)), dma((pairs, 4, 2)), dma((3,)), dma((3,)),
            dma((pairs, 2, 2)), dma((pairs, 2, 2)), dma((pairs, 2)), dma((pairs, 2)),
            dma((pairs, 4)), dma((pairs, 4)), dma((pairs,)), dma((pairs,)),
            dma((2, heads, 5)), dma((2, heads, 5)), dma((2, heads, 3)), dma((2, heads, 3)),
            dma((1,)), dma((1,)), dma((1,)),
        ],
        compiler_params=pltpu.CompilerParams(
            collective_id=0, has_side_effects=True, vmem_limit_bytes=58 * 1024 * 1024
        ),
    )(latent, w_qkv, mod_shift, mod_scale, attn_gate, qk_gain, slot_tile, window_tiles)


def solution(mesh, nx=NX):
    return jax.shard_map(
        functools.partial(on_device, nx),
        mesh=mesh,
        in_specs=(
            P(None, "tile", None),
            P("section", "tile", None),
            P("section", None),
            P("section", None),
            P("section", None),
            P("section", None),
            P(),
            P(),
        ),
        out_specs=P("section", None, "tile", None),
        check_vma=False,
    )
```

```python
import functools
import math

import jax
import jax.numpy as jnp
from jax import lax
from jax.experimental import pallas as pl
from jax.experimental.pallas import tpu as pltpu
from jax.sharding import PartitionSpec as P

MESH = pl.DeviceIdType.MESH
HEAD = 128
SLOTS = 3
NY = 4
NX = 4
EPS = 1e-06
NEG = -1e30


def kernel(
    layers, nx, nz, heads, tokens, lat, w_part, shift_row, scale_row, gate_row, gain_row, slot_ids, windows, out,
    hbuf, mod, wbuf, parbuf, qbuf, kvo, kvn, acc, bias,
    loc_sem, a2a_s, a2a_r, par_s, par_r, z_s, z_r, x0_s, x0_r, x_s, x_r, xf_s, xf_r, c_s, c_r, cp_s, cp_r,
    kv_s, kv_r, g_s, g_r, o_s, o_r, o_l,
):
    width = NY * heads * HEAD
    half = tokens // 2
    chunk = half // SLOTS
    shard = w_part.shape[1]
    group = heads * HEAD
    n_tile = nx * nz
    section = lax.axis_index("section")
    t = lax.axis_index("tile")
    y, c = section // 2, section % 2
    x, z = t // nz, t % nz
    sib = (2 * y + 1 - c, t)
    t_next = (section, (t + 1) % n_tile)
    t_prev = (section, (t + n_tile - 1) % n_tile)
    x_next = (section, ((x + 1) % nx) * nz + z)
    x_prev = (section, ((x + nx - 1) % nx) * nz + z)

    def y_peer(d):
        return (2 * ((y + d) % NY) + c, t)

    z_order = []
    for d in range(1, nz // 2 + 1):
        z_order += [d] if 2 * d == nz else [d, nz - d]

    def z_peer(d):
        return (section, x * nz + (z + d) % nz)

    def remote(src, dst, send, recv, device):
        return pltpu.make_async_remote_copy(
            src_ref=src, dst_ref=dst, send_sem=send, recv_sem=recv, device_id=device, device_id_type=MESH
        )

    partners = [y_peer(1), y_peer(2), y_peer(3), sib, t_next, t_prev]
    partners += [z_peer(d) for d in z_order]
    if nx > 1:
        partners += [x_next, x_prev, (section, ((x + 2) % nx) * nz + z)]
    load_h = pltpu.make_async_copy(lat.at[0, pl.ds(pl.multiple_of(half * c, 16), half)], hbuf.at[0], loc_sem.at[0])
    load_h.start()
    own_rows = pl.ds(pl.multiple_of(shard * t, 16), shard)

    def w_slices(place):
        for i in range(3):
            start = pl.multiple_of(i * width + place * group, HEAD)
            yield w_part.at[0, :, pl.ds(start, group)], wbuf.at[section, own_rows, i * group : (i + 1) * group]

    own_shard = wbuf.at[section, own_rows]
    for src, dst in w_slices(y):
        pltpu.make_async_copy(src, dst, loc_sem.at[1]).start()
    parbuf[section] = jnp.zeros(parbuf.shape[1:], jnp.float32)
    for i, row in enumerate((shift_row, scale_row, gate_row)):
        parbuf[section, i : i + 1, :] = row[...]
    parbuf[section, 3:4, 0:HEAD] = gain_row[...]
    barrier = pltpu.get_barrier_semaphore()
    for device in partners:
        pl.semaphore_signal(barrier, inc=1, device_id=device, device_id_type=MESH)
    pl.semaphore_wait(barrier, len(partners))

    def a2a_start():
        for d in (1, 3, 2):
            for src, dst in w_slices((y + d) % NY):
                remote(src, dst, a2a_s.at[d - 1], a2a_r.at[d - 1], y_peer(d)).start()
            remote(parbuf.at[section], parbuf.at[section], par_s.at[d - 1], par_r.at[d - 1], y_peer(d)).start()

    def a2a_whole(d):
        return (
            remote(own_shard, own_shard, a2a_s.at[d - 1], a2a_r.at[d - 1], sib),
            remote(parbuf.at[section], parbuf.at[section], par_s.at[d - 1], par_r.at[d - 1], sib),
        )

    @pl.when(y == 0)
    def _():
        a2a_start()

    @pl.when(y != 0)
    def _():
        for copy in a2a_whole(y):
            copy.wait_recv()
        a2a_start()

    pltpu.make_async_copy(own_shard, own_shard, loc_sem.at[1]).wait()

    def a2a_finish():
        for d in (1, 2, 3):
            for copy in a2a_whole(d):
                copy.wait_send()

            @pl.when(d != y)
            def _():
                for copy in a2a_whole(d):
                    copy.wait_recv()

    def rows_of(xx, zz):
        return pl.ds(pl.multiple_of((xx * nz + zz) * shard, 16), shard)

    def z_copy(layer, d, back=False):
        k = layer // 2
        ref = wbuf.at[layer, rows_of(x, (z + nz - d) % nz if back else z)]
        return remote(ref, ref, z_s.at[k, d - 1], z_r.at[k, d - 1], z_peer(d))

    def z_start(layer, order=None):
        for d in z_order if order is None else order:
            z_copy(layer, d).start()

    def z_finish(layer):
        for d in z_order:
            z_copy(layer, d, True).wait_recv()
        for d in z_order:
            z_copy(layer, d).wait_send()

    block = nz * shard

    def x_rows(place, piece=None):
        if piece is None:
            return pl.ds(pl.multiple_of(place * block, 16), block)
        return pl.ds(pl.multiple_of(place * block + piece * (block // 2), 16), block // 2)

    def x_copy(layer, way, order):
        ref = wbuf.at[layer, x_rows(x, order if way == 0 else 1 - order)]
        k = layer // 2
        return remote(ref, ref, x_s.at[k, way, order], x_r.at[k, way, order], x_next if way == 0 else x_prev)

    def x_forward(layer, way):
        place = (x + nx - 1) % nx if way == 0 else (x + 1) % nx
        ref = wbuf.at[layer, x_rows(place, way)]
        k = layer // 2
        return remote(ref, ref, xf_s.at[k, way], xf_r.at[k, way], x_next if way == 0 else x_prev)

    def core_copy(layer, d):
        k = layer // 2
        ref = wbuf.at[layer, x_rows((x + d) % nx)]
        return remote(ref, ref, c_s.at[k, d], c_r.at[k, d], sib)

    def core_par(layer):
        k = layer // 2
        return remote(parbuf.at[layer], parbuf.at[layer], cp_s.at[k], cp_r.at[k], sib)

    def x_event(layer, step):
        if step == 2:
            core_copy(layer, 0).start()
            core_par(layer).start()
        if nx == 1:
            return
        if step == 0:
            for order in range(2):
                for way in range(2):
                    x_copy(layer, way, order).start()
        elif step == 1:
            for way in range(2):
                x_copy(layer, way, 0).wait_recv()
                x_forward(layer, way).start()
        else:
            for way in range(2):
                x_copy(layer, way, 1).wait_recv()
                core_copy(layer, nx - 1 if way == 0 else 1).start()
            for way in range(2):
                x_forward(layer, way).wait_recv()
            core_copy(layer, 2).start()
            for way in range(2):
                x_copy(layer, way, 0).wait_send()
                x_copy(layer, way, 1).wait_send()
                x_forward(layer, way).wait_send()

    def x_direct(zz):
        ref = wbuf.at[0, rows_of(x, zz)]
        for d in (1, 3, 2) if nx == 4 else ():
            to = (section, ((x + d) % nx) * nz + z)
            remote(ref, ref, x0_s.at[d - 1], x0_r.at[d - 1], to).start()

    def x_direct_whole(d, back):
        ref = wbuf.at[0, x_rows((x + nx - d) % nx if back else x)]
        return remote(ref, ref, x0_s.at[d - 1], x0_r.at[d - 1], sib)

    @pl.when(c == 0)
    def _():
        z_start(0)
        x_direct(z)
        for d in z_order:
            z_copy(0, d, True).wait_recv()
            x_direct((z + nz - d) % nz)
        core_copy(0, 0).start()
        core_par(0).start()
        for d in z_order:
            z_copy(0, d).wait_send()
        a2a_finish()
        z_start(2)
        if nx > 1:
            for d in (1, 3, 2):
                x_direct_whole(d, True).wait_recv()
                core_copy(0, nx - d).start()
            for d in (1, 3, 2):
                x_direct_whole(d, False).wait_send()

    @pl.when(c == 1)
    def _():
        z_start(1)
        a2a_finish()
        core_copy(0, 0).wait_recv()
        core_par(0).wait_recv()
        for d in range(1, nx):
            core_copy(0, d).wait_recv()
        z_finish(1)
        x_event(1, 0)

    tile_len = tokens // SLOTS
    n_slots = n_tile * SLOTS
    lanes = lax.broadcasted_iota(jnp.int32, (1, tokens), 1)

    def penalty(query_slot, frame, key_slot):
        place = (t + n_tile + frame) % n_tile
        key_id = slot_ids[place * SLOTS + key_slot]
        row = windows[pl.ds(slot_ids[t * SLOTS + query_slot], 1), :]
        listed = jnp.max(jnp.where(row == key_id, 1.0, 0.0), axis=1, keepdims=True)
        return jnp.where(listed > 0.0, 0.0, NEG)

    for i in range(SLOTS):
        query_slot = (half * c + chunk * i) // tile_len
        table = [[penalty(query_slot, frame, k) for k in range(SLOTS)] for frame in (-1, 0, 1)]

        def spread_over(tokens_at, pens):
            return jnp.where(tokens_at < tile_len, pens[0], jnp.where(tokens_at < 2 * tile_len, pens[1], pens[2]))

        bias[0, i] = spread_over(lanes, table[1])
        for side in range(2):
            low = spread_over(lanes + side * half, table[0])
            high = spread_over(lanes - half + side * half, table[2])
            bias[1 + side, i] = jnp.where(lanes < half, low, high)

    load_h.wait()

    ones = jnp.ones((tokens, HEAD), jnp.bfloat16)

    def dot(a, b):
        return jnp.dot(a, b, preferred_element_type=jnp.float32)

    def head_norm(numbers, gain):
        square_mean = jnp.mean(numbers * numbers, axis=-1, keepdims=True)
        return (numbers * lax.rsqrt(square_mean + EPS) * gain).astype(jnp.bfloat16)

    def one_block(j, keys, values, allowed):
        scores = lax.dot_general(
            qbuf[j], keys, (((1,), (1,)), ((), ())), preferred_element_type=jnp.float32
        )
        scores = scores.reshape(SLOTS, chunk, tokens) + allowed
        powers = jnp.exp2(scores).astype(jnp.bfloat16).reshape(half, tokens)
        return dot(powers, jnp.concatenate([values, ones], axis=1))

    def layer_step(layer, carry):
        p = layer % 2
        q = 1 - p

        def event(ahead, condition, do):
            ours = jnp.logical_and((layer + ahead) % 2 == c, layer + ahead < layers)
            if condition is not None:
                ours = jnp.logical_and(ours, condition)

            @pl.when(ours)
            def _():
                do(layer + ahead)

        def z_then_x(target):
            z_finish(target)
            x_event(target, 0)

        def at(place):
            if place == 0:
                event(1, layer > 0, lambda target: x_event(target, 1))
            if place == 1:
                event(1, layer == 0, lambda target: x_event(target, 1))
                event(2, None, z_then_x)
            if place == 2:
                event(3, None, z_start)
                event(1, None, lambda target: x_event(target, 2))

        @pl.when(jnp.logical_and(c != p, layer > 0))
        def _():
            core_par(layer).wait_recv()
            for d in range(nx):
                core_copy(layer, d).wait_recv()

        shifts = parbuf[layer, 0:1, :]
        scales = parbuf[layer, 1:2, :]
        gain = parbuf[layer, 3:4, 0:HEAD]
        for i in range(SLOTS):
            rows = pl.ds(i * chunk, chunk)
            numbers = hbuf[p, rows, :].astype(jnp.float32)
            average = jnp.mean(numbers, axis=-1, keepdims=True)
            centred = numbers - average
            spread = jnp.mean(centred * centred, axis=-1, keepdims=True)
            mod[rows, :] = (centred * lax.rsqrt(spread + EPS) * scales + shifts).astype(jnp.bfloat16)

        def kv_copy(j, kind):
            if kind == 0:
                ref = kvo.at[p, j, c]
                dst, device = ref, sib
            elif kind == 1:
                ref, dst, device = kvo.at[p, j, c], kvn.at[p, j, c, 0], t_next
            elif kind == 2:
                ref, dst, device = kvo.at[p, j, c], kvn.at[p, j, c, 1], t_prev
            else:
                ref = kvn.at[p, j, c, kind - 3]
                dst, device = ref, sib
            return remote(ref, dst, kv_s.at[p, j, kind], kv_r.at[p, j, kind], device)

        for j in range(heads):
            weights = jnp.concatenate(
                [wbuf[layer, :, i * group + HEAD * j : i * group + HEAD * (j + 1)] for i in (1, 2)], axis=1
            )
            projected = dot(mod[...], weights)
            kvo[p, j, c, :, 0:HEAD] = head_norm(projected[:, 0:HEAD], gain)
            kvo[p, j, c, :, HEAD : 2 * HEAD] = projected[:, HEAD:].astype(jnp.bfloat16)
            for kind in (1, 2, 0):
                kv_copy(j, kind).start()
        at(0)
        queries = dot(mod[...], wbuf[layer, :, 0:group])
        query_gain = gain * (math.log2(math.e) / math.sqrt(HEAD))
        for j in range(heads):
            qbuf[j] = head_norm(queries[:, HEAD * j : HEAD * (j + 1)], query_gain)

        @pl.when(section == layer - 1)
        def _():
            keep_own().wait()

        @pl.when(2 * y + 1 - c == layer - 1)
        def _():
            keep_other().wait_send()

        for j in range(heads):
            kv_copy(j, 0).wait_recv()
            block = kvo[p, j].reshape(tokens, 2 * HEAD)
            acc[j] = one_block(j, block[:, 0:HEAD], block[:, HEAD:], bias[0])

        def near(j, side):
            block = kvn[p, j, side].reshape(tokens, 2 * HEAD)
            return one_block(j, block[:, 0:HEAD], block[:, HEAD:], bias[1 + side])

        def pass_on(j):
            for kind in (1, 2):
                kv_copy(j, kind).wait_recv()
                kv_copy(j, kind + 2).start()
            acc[j] += near(j, c)

        def g_copy(j, d, back):
            place = (y + NY - d) % NY if back else y
            columns = pl.ds(pl.multiple_of((place * heads + j) * HEAD, HEAD), HEAD)
            ref = hbuf.at[q, :, columns]
            return remote(ref, ref, g_s.at[p, j, d - 1], g_r.at[p, j, d - 1], y_peer(d))

        def sends_to(d):
            return jnp.logical_or(layer < layers - 1, (y + d) % NY == NY - 1)

        def finish(j):
            for kind in (3, 4):
                kv_copy(j, kind).wait_recv()
            total = acc[j] + near(j, 1 - c)
            columns = pl.ds(pl.multiple_of((y * heads + j) * HEAD, HEAD), HEAD)
            attended = total[:, 0:HEAD] / total[:, HEAD:]
            gates = parbuf[layer, 2:3, columns]
            numbers = hbuf[p, :, columns].astype(jnp.float32) + gates * attended
            hbuf[q, :, columns] = numbers.astype(jnp.bfloat16)
            for d in (1, 3, 2):

                @pl.when(sends_to(d))
                def _():
                    g_copy(j, d, False).start()

        for j in range(heads):
            pass_on(j)
            finish(j)
            if j == 0:
                at(1)
        at(2)
        for j in range(heads):
            for kind in range(5):
                kv_copy(j, kind).wait_send()
        for d in (1, 3, 2):

            @pl.when(sends_to(d))
            def _():
                for j in range(heads):
                    g_copy(j, d, False).wait_send()

        @pl.when(sends_to(0))
        def _():
            for j in range(heads):
                for d in (1, 3, 2):
                    g_copy(j, d, True).wait_recv()

        @pl.when(c == p)
        def _():
            core_par(layer).wait_send()
            for d in range(nx):
                core_copy(layer, d).wait_send()

        @pl.when(section == layer)
        def _():
            keep_own().start()

        @pl.when(2 * y + 1 - c == layer)
        def _():
            keep_other().start()

        return carry

    def out_rows(place):
        return out.at[0, 0, pl.ds(pl.multiple_of(half * place, 16), half)]

    def keep_own():
        return pltpu.make_async_copy(hbuf.at[1 - c], out_rows(c), o_l.at[0])

    def keep_other():
        return remote(hbuf.at[c], out_rows(c), o_s.at[0], o_r.at[0], sib)

    lax.fori_loop(0, layers, layer_step, 0)

    @pl.when(section == layers - 1)
    def _():
        keep_own().wait()

    @pl.when(2 * y + 1 - c == layers - 1)
    def _():
        keep_other().wait_send()

    remote(hbuf.at[c], out_rows(1 - c), o_s.at[0], o_r.at[0], sib).wait_recv()


def on_device(nx, latent, w_qkv, mod_shift, mod_scale, attn_gate, qk_gain, slot_tile, window_tiles):
    layers = lax.axis_size("section")
    n_tile = lax.axis_size("tile")
    nz = n_tile // nx
    _, tokens, width = latent.shape
    heads = width // HEAD // NY
    shard = w_qkv.shape[1]
    half = tokens // 2
    cols = 3 * heads * HEAD
    pairs = layers // 2
    bf16, f32 = jnp.bfloat16, jnp.float32
    dma = pltpu.SemaphoreType.DMA
    any_space = pl.BlockSpec(memory_space=pl.ANY)
    in_vmem = pl.BlockSpec(memory_space=pltpu.VMEM)
    return pl.pallas_call(
        functools.partial(kernel, layers, nx, nz, heads, tokens),
        out_shape=jax.ShapeDtypeStruct((1, 1, tokens, width), bf16),
        in_specs=[any_space, any_space] + [in_vmem] * 4 + [pl.BlockSpec(memory_space=pltpu.SMEM), in_vmem],
        out_specs=any_space,
        scratch_shapes=[
            pltpu.VMEM((2, half, width), bf16),
            pltpu.VMEM((half, width), bf16),
            pltpu.VMEM((layers, width, cols), bf16),
            pltpu.VMEM((layers, 8, width), f32),
            pltpu.VMEM((heads, half, HEAD), bf16),
            pltpu.VMEM((2, heads, 2, half, 2 * HEAD), bf16),
            pltpu.VMEM((2, heads, 2, 2, half, 2 * HEAD), bf16),
            pltpu.VMEM((heads, half, 2 * HEAD), f32),
            pltpu.VMEM((3, SLOTS, 1, tokens), f32),
            dma((3,)), dma((3,)), dma((3,)), dma((3,)), dma((3,)),
            dma((pairs, 8)), dma((pairs, 8)), dma((3,)), dma((3,)),
            dma((pairs, 2, 2)), dma((pairs, 2, 2)), dma((pairs, 2)), dma((pairs, 2)),
            dma((pairs, 4)), dma((pairs, 4)), dma((pairs,)), dma((pairs,)),
            dma((2, heads, 5)), dma((2, heads, 5)), dma((2, heads, 3)), dma((2, heads, 3)),
            dma((1,)), dma((1,)), dma((1,)),
        ],
        compiler_params=pltpu.CompilerParams(
            collective_id=0, has_side_effects=True, vmem_limit_bytes=58 * 1024 * 1024
        ),
    )(latent, w_qkv, mod_shift, mod_scale, attn_gate, qk_gain, slot_tile, window_tiles)


def solution(mesh, nx=NX):
    return jax.shard_map(
        functools.partial(on_device, nx),
        mesh=mesh,
        in_specs=(
            P(None, "tile", None),
            P("section", "tile", None),
            P("section", None),
            P("section", None),
            P("section", None),
            P("section", None),
            P(),
            P(),
        ),
        out_specs=P("section", None, "tile", None),
        check_vma=False,
    )
```

```python
import functools
import math

import jax
import jax.numpy as jnp
from jax import lax
from jax.experimental import pallas as pl
from jax.experimental.pallas import tpu as pltpu
from jax.sharding import PartitionSpec as P

MESH = pl.DeviceIdType.MESH
HEAD = 128
SLOTS = 3
NY = 4
NX = 4
EPS = 1e-06
NEG = -1e30


def kernel(
    layers, nx, nz, heads, tokens, lat, w_part, shift_row, scale_row, gate_row, gain_row, slot_ids, windows, out,
    hbuf, mod, wbuf, parbuf, qbuf, kvo, kvn, acc, bias,
    loc_sem, a2a_s, a2a_r, par_s, par_r, z_s, z_r, x0_s, x0_r, x_s, x_r, xf_s, xf_r, c_s, c_r, cp_s, cp_r,
    kv_s, kv_r, g_s, g_r, o_s, o_r, o_l,
):
    width = NY * heads * HEAD
    half = tokens // 2
    chunk = half // SLOTS
    shard = w_part.shape[1]
    group = heads * HEAD
    n_tile = nx * nz
    section = lax.axis_index("section")
    t = lax.axis_index("tile")
    y, c = section // 2, section % 2
    x, z = t // nz, t % nz
    sib = (2 * y + 1 - c, t)
    t_next = (section, (t + 1) % n_tile)
    t_prev = (section, (t + n_tile - 1) % n_tile)
    x_next = (section, ((x + 1) % nx) * nz + z)
    x_prev = (section, ((x + nx - 1) % nx) * nz + z)

    def y_peer(d):
        return (2 * ((y + d) % NY) + c, t)

    z_order = []
    for d in range(1, nz // 2 + 1):
        z_order += [d] if 2 * d == nz else [d, nz - d]

    def z_peer(d):
        return (section, x * nz + (z + d) % nz)

    def remote(src, dst, send, recv, device):
        return pltpu.make_async_remote_copy(
            src_ref=src, dst_ref=dst, send_sem=send, recv_sem=recv, device_id=device, device_id_type=MESH
        )

    partners = [y_peer(1), y_peer(2), y_peer(3), sib, t_next, t_prev]
    partners += [z_peer(d) for d in z_order]
    if nx > 1:
        partners += [x_next, x_prev, (section, ((x + 2) % nx) * nz + z)]
    load_h = pltpu.make_async_copy(lat.at[0, pl.ds(pl.multiple_of(half * c, 16), half)], hbuf.at[0], loc_sem.at[0])
    load_h.start()
    own_rows = pl.ds(pl.multiple_of(shard * t, 16), shard)

    def w_slices(place):
        for i in range(3):
            start = pl.multiple_of(i * width + place * group, HEAD)
            yield w_part.at[0, :, pl.ds(start, group)], wbuf.at[section, own_rows, i * group : (i + 1) * group]

    own_shard = wbuf.at[section, own_rows]
    for src, dst in w_slices(y):
        pltpu.make_async_copy(src, dst, loc_sem.at[1]).start()
    parbuf[section] = jnp.zeros(parbuf.shape[1:], jnp.float32)
    for i, row in enumerate((shift_row, scale_row, gate_row)):
        parbuf[section, i : i + 1, :] = row[...]
    parbuf[section, 3:4, 0:HEAD] = gain_row[...]
    barrier = pltpu.get_barrier_semaphore()
    for device in partners:
        pl.semaphore_signal(barrier, inc=1, device_id=device, device_id_type=MESH)
    pl.semaphore_wait(barrier, len(partners))

    def a2a_start():
        for d in (1, 3, 2):
            for src, dst in w_slices((y + d) % NY):
                remote(src, dst, a2a_s.at[d - 1], a2a_r.at[d - 1], y_peer(d)).start()
            remote(parbuf.at[section], parbuf.at[section], par_s.at[d - 1], par_r.at[d - 1], y_peer(d)).start()

    def a2a_whole(d):
        return (
            remote(own_shard, own_shard, a2a_s.at[d - 1], a2a_r.at[d - 1], sib),
            remote(parbuf.at[section], parbuf.at[section], par_s.at[d - 1], par_r.at[d - 1], sib),
        )

    @pl.when(y == 0)
    def _():
        a2a_start()

    @pl.when(y != 0)
    def _():
        for copy in a2a_whole(y):
            copy.wait_recv()
        a2a_start()

    pltpu.make_async_copy(own_shard, own_shard, loc_sem.at[1]).wait()

    def a2a_finish():
        for d in (1, 2, 3):
            for copy in a2a_whole(d):
                copy.wait_send()

            @pl.when(d != y)
            def _():
                for copy in a2a_whole(d):
                    copy.wait_recv()

    def rows_of(xx, zz):
        return pl.ds(pl.multiple_of((xx * nz + zz) * shard, 16), shard)

    def z_copy(layer, d, back=False):
        k = layer // 2
        ref = wbuf.at[layer, rows_of(x, (z + nz - d) % nz if back else z)]
        return remote(ref, ref, z_s.at[k, d - 1], z_r.at[k, d - 1], z_peer(d))

    def z_start(layer, order=None):
        for d in z_order if order is None else order:
            z_copy(layer, d).start()

    def z_finish(layer):
        for d in z_order:
            z_copy(layer, d, True).wait_recv()
        for d in z_order:
            z_copy(layer, d).wait_send()

    block = nz * shard

    def x_rows(place, piece=None):
        if piece is None:
            return pl.ds(pl.multiple_of(place * block, 16), block)
        return pl.ds(pl.multiple_of(place * block + piece * (block // 2), 16), block // 2)

    def x_copy(layer, way, order):
        ref = wbuf.at[layer, x_rows(x, order if way == 0 else 1 - order)]
        k = layer // 2
        return remote(ref, ref, x_s.at[k, way, order], x_r.at[k, way, order], x_next if way == 0 else x_prev)

    def x_forward(layer, part, way):
        place = (x + nx - 1) % nx if way == 0 else (x + 1) % nx
        ref = wbuf.at[layer, x_rows(place, part)]
        k = layer // 2
        return remote(ref, ref, xf_s.at[k, part], xf_r.at[k, part], x_next if way == 0 else x_prev)

    def x_forward_early(layer):
        for way in range(2 if nx > 1 else 0):
            x_copy(layer, way, 0).wait_recv()

            @pl.when(z != (0 if way == 0 else nz - 1))
            def _():
                x_forward(layer, way, way).start()

    def x_forward_late(layer):
        for way in range(2 if nx > 1 else 0):

            @pl.when(z == (nz - 1 if way == 0 else 0))
            def _():
                x_copy(layer, way, 1).wait_recv()
                x_forward(layer, 1 - way, way).start()

    def core_copy(layer, d):
        k = layer // 2
        ref = wbuf.at[layer, x_rows((x + d) % nx)]
        return remote(ref, ref, c_s.at[k, d], c_r.at[k, d], sib)

    def core_par(layer):
        k = layer // 2
        return remote(parbuf.at[layer], parbuf.at[layer], cp_s.at[k], cp_r.at[k], sib)

    def x_event(layer):
        if nx > 1:
            for order in range(2):
                for way in range(2):
                    x_copy(layer, way, order).start()

    def core_first(layer):
        core_copy(layer, 0).start()
        core_par(layer).start()

    def core_second(layer):
        if nx > 1:
            for way in range(2):

                @pl.when(z != (nz - 1 if way == 0 else 0))
                def _():
                    x_copy(layer, way, 1).wait_recv()

                core_copy(layer, nx - 1 if way == 0 else 1).start()

    def core_last(layer):
        if nx > 1:
            for part in range(2):
                x_forward(layer, part, 0).wait_recv()
            core_copy(layer, 2).start()
            for part in range(2):
                x_copy(layer, 0, part).wait_send()
                x_copy(layer, 1, part).wait_send()
            for part in range(2):
                x_forward(layer, part, 0).wait_send()

    def x_direct(zz):
        ref = wbuf.at[0, rows_of(x, zz)]
        for d in (1, 3, 2) if nx == 4 else ():
            to = (section, ((x + d) % nx) * nz + z)
            remote(ref, ref, x0_s.at[d - 1], x0_r.at[d - 1], to).start()

    def x_direct_whole(d, back):
        ref = wbuf.at[0, x_rows((x + nx - d) % nx if back else x)]
        return remote(ref, ref, x0_s.at[d - 1], x0_r.at[d - 1], sib)

    @pl.when(c == 0)
    def _():
        z_start(0)
        x_direct(z)
        for d in z_order:
            z_copy(0, d, True).wait_recv()
            x_direct((z + nz - d) % nz)
        core_copy(0, 0).start()
        core_par(0).start()
        for d in z_order:
            z_copy(0, d).wait_send()
        a2a_finish()
        if nx > 1:
            for d in (1, 3, 2):
                x_direct_whole(d, True).wait_recv()
                core_copy(0, nx - d).start()
            for d in (1, 3, 2):
                x_direct_whole(d, False).wait_send()

    @pl.when(c == 1)
    def _():
        a2a_finish()
        core_copy(0, 0).wait_recv()
        core_par(0).wait_recv()
        z_start(1)
        for d in range(1, nx):
            core_copy(0, d).wait_recv()

    tile_len = tokens // SLOTS
    n_slots = n_tile * SLOTS
    lanes = lax.broadcasted_iota(jnp.int32, (1, tokens), 1)

    tile_lanes = lax.broadcasted_iota(jnp.int32, windows.shape, 1)

    def penalty(query_slot, frame, key_slot):
        place = (t + n_tile + frame) % n_tile
        key_id = slot_ids[place * SLOTS + key_slot]
        in_window = jnp.logical_and(tile_lanes == slot_ids[t * SLOTS + query_slot], windows[...] == key_id)
        listed = jnp.max(jnp.where(in_window, 1.0, 0.0), axis=(0, 1), keepdims=True)
        return jnp.where(listed > 0.0, 0.0, NEG)

    for i in range(SLOTS):
        query_slot = (half * c + chunk * i) // tile_len
        table = [[penalty(query_slot, frame, k) for k in range(SLOTS)] for frame in (-1, 0, 1)]

        def spread_over(tokens_at, pens):
            return jnp.where(tokens_at < tile_len, pens[0], jnp.where(tokens_at < 2 * tile_len, pens[1], pens[2]))

        bias[0, i] = spread_over(lanes, table[1])
        for side in range(2):
            low = spread_over(lanes + side * half, table[0])
            high = spread_over(lanes - half + side * half, table[2])
            bias[1 + side, i] = jnp.where(lanes < half, low, high)

    load_h.wait()

    ones = jnp.ones((tokens, HEAD), jnp.bfloat16)

    def dot(a, b):
        return jnp.dot(a, b, preferred_element_type=jnp.float32)

    def head_norm(numbers, gain):
        square_mean = jnp.mean(numbers * numbers, axis=-1, keepdims=True)
        return (numbers * lax.rsqrt(square_mean + EPS) * gain).astype(jnp.bfloat16)

    def one_block(j, keys, values, allowed):
        scores = lax.dot_general(
            qbuf[j], keys, (((1,), (1,)), ((), ())), preferred_element_type=jnp.float32
        )
        scores = scores.reshape(SLOTS, chunk, tokens) + allowed
        powers = jnp.exp2(scores).astype(jnp.bfloat16).reshape(half, tokens)
        return dot(powers, jnp.concatenate([values, ones], axis=1))

    def layer_step(layer, carry):
        p = layer % 2
        q = 1 - p

        def event(ahead, condition, do):
            ours = jnp.logical_and((layer + ahead) % 2 == c, layer + ahead < layers)
            if condition is not None:
                ours = jnp.logical_and(ours, condition)

            @pl.when(ours)
            def _():
                do(layer + ahead)

        def z_then_x(target):
            z_finish(target)
            x_event(target)

        def middle(target):
            x_forward_late(target)
            core_second(target)

        def first_end(target):
            x_forward_late(target)
            core_first(target)
            core_second(target)

        def at(place):
            if place == 0:
                event(1, layer == 0, z_then_x)
                event(1, layer > 1, x_forward_early)
                event(1, layer > 1, core_first)
            elif place == 1:
                event(1, layer > 1, middle)
            elif place == 2:
                event(1, layer <= 1, x_forward_early)
                event(2, layer > 0, z_then_x)
                event(2, layer == 0, z_start)
            elif place == 3:
                event(3, None, z_start)
            else:
                event(1, layer <= 1, first_end)
                event(1, None, core_last)
                event(2, layer == 0, z_then_x)

        @pl.when(jnp.logical_and(c != p, layer > 0))
        def _():
            core_par(layer).wait_recv()
            for d in range(nx):
                core_copy(layer, d).wait_recv()

        shifts = parbuf[layer, 0:1, :]
        scales = parbuf[layer, 1:2, :]
        gain = parbuf[layer, 3:4, 0:HEAD]
        for i in range(SLOTS):
            rows = pl.ds(i * chunk, chunk)
            numbers = hbuf[p, rows, :].astype(jnp.float32)
            average = jnp.mean(numbers, axis=-1, keepdims=True)
            centred = numbers - average
            spread = jnp.mean(centred * centred, axis=-1, keepdims=True)
            mod[rows, :] = (centred * lax.rsqrt(spread + EPS) * scales + shifts).astype(jnp.bfloat16)

        def kv_copy(j, kind):
            if kind == 0:
                ref = kvo.at[p, j, c]
                dst, device = ref, sib
            elif kind == 1:
                ref, dst, device = kvo.at[p, j, c], kvn.at[p, j, c, 0], t_next
            elif kind == 2:
                ref, dst, device = kvo.at[p, j, c], kvn.at[p, j, c, 1], t_prev
            else:
                ref = kvn.at[p, j, c, kind - 3]
                dst, device = ref, sib
            return remote(ref, dst, kv_s.at[p, j, kind], kv_r.at[p, j, kind], device)

        for j in range(heads):
            weights = jnp.concatenate(
                [wbuf[layer, :, i * group + HEAD * j : i * group + HEAD * (j + 1)] for i in (1, 2)], axis=1
            )
            projected = dot(mod[...], weights)
            kvo[p, j, c, :, 0:HEAD] = head_norm(projected[:, 0:HEAD], gain)
            kvo[p, j, c, :, HEAD : 2 * HEAD] = projected[:, HEAD:].astype(jnp.bfloat16)
            for kind in (1, 2, 0):
                kv_copy(j, kind).start()
        at(0)
        queries = dot(mod[...], wbuf[layer, :, 0:group])
        query_gain = gain * (math.log2(math.e) / math.sqrt(HEAD))
        for j in range(heads):
            qbuf[j] = head_norm(queries[:, HEAD * j : HEAD * (j + 1)], query_gain)

        @pl.when(section == layer - 1)
        def _():
            keep_own().wait()

        @pl.when(2 * y + 1 - c == layer - 1)
        def _():
            keep_other().wait_send()

        for j in range(heads):
            kv_copy(j, 0).wait_recv()
            block = kvo[p, j].reshape(tokens, 2 * HEAD)
            acc[j] = one_block(j, block[:, 0:HEAD], block[:, HEAD:], bias[0])
        at(1)

        def near(j, side):
            block = kvn[p, j, side].reshape(tokens, 2 * HEAD)
            return one_block(j, block[:, 0:HEAD], block[:, HEAD:], bias[1 + side])

        def pass_on(j):
            for kind in (1, 2):
                kv_copy(j, kind).wait_recv()
                kv_copy(j, kind + 2).start()
            acc[j] += near(j, c)

        def g_copy(j, d, back):
            place = (y + NY - d) % NY if back else y
            columns = pl.ds(pl.multiple_of((place * heads + j) * HEAD, HEAD), HEAD)
            ref = hbuf.at[q, :, columns]
            return remote(ref, ref, g_s.at[p, j, d - 1], g_r.at[p, j, d - 1], y_peer(d))

        def sends_to(d):
            return jnp.logical_or(layer < layers - 1, (y + d) % NY == NY - 1)

        def finish(j):
            for kind in (3, 4):
                kv_copy(j, kind).wait_recv()
            total = acc[j] + near(j, 1 - c)
            columns = pl.ds(pl.multiple_of((y * heads + j) * HEAD, HEAD), HEAD)
            attended = total[:, 0:HEAD] / total[:, HEAD:]
            gates = parbuf[layer, 2:3, columns]
            numbers = hbuf[p, :, columns].astype(jnp.float32) + gates * attended
            hbuf[q, :, columns] = numbers.astype(jnp.bfloat16)
            for d in (1, 3, 2):

                @pl.when(sends_to(d))
                def _():
                    g_copy(j, d, False).start()

        for j in range(heads):
            pass_on(j)
            if j == heads - 1:
                at(3)
            finish(j)
            if j == 0:
                at(2)
        at(4)
        for j in range(heads):
            for kind in range(5):
                kv_copy(j, kind).wait_send()
        for d in (1, 3, 2):

            @pl.when(sends_to(d))
            def _():
                for j in range(heads):
                    g_copy(j, d, False).wait_send()

        @pl.when(sends_to(0))
        def _():
            for j in range(heads):
                for d in (1, 3, 2):
                    g_copy(j, d, True).wait_recv()

        @pl.when(c == p)
        def _():
            core_par(layer).wait_send()
            for d in range(nx):
                core_copy(layer, d).wait_send()

        @pl.when(section == layer)
        def _():
            keep_own().start()

        @pl.when(2 * y + 1 - c == layer)
        def _():
            keep_other().start()

        return carry

    def out_rows(place):
        return out.at[0, 0, pl.ds(pl.multiple_of(half * place, 16), half)]

    def keep_own():
        return pltpu.make_async_copy(hbuf.at[1 - c], out_rows(c), o_l.at[0])

    def keep_other():
        return remote(hbuf.at[c], out_rows(c), o_s.at[0], o_r.at[0], sib)

    lax.fori_loop(0, layers, layer_step, 0)

    @pl.when(section == layers - 1)
    def _():
        keep_own().wait()

    @pl.when(2 * y + 1 - c == layers - 1)
    def _():
        keep_other().wait_send()

    remote(hbuf.at[c], out_rows(1 - c), o_s.at[0], o_r.at[0], sib).wait_recv()


def on_device(nx, latent, w_qkv, mod_shift, mod_scale, attn_gate, qk_gain, slot_tile, window_tiles):
    layers = lax.axis_size("section")
    n_tile = lax.axis_size("tile")
    nz = n_tile // nx
    _, tokens, width = latent.shape
    heads = width // HEAD // NY
    shard = w_qkv.shape[1]
    half = tokens // 2
    cols = 3 * heads * HEAD
    pairs = layers // 2
    bf16, f32 = jnp.bfloat16, jnp.float32
    dma = pltpu.SemaphoreType.DMA
    any_space = pl.BlockSpec(memory_space=pl.ANY)
    in_vmem = pl.BlockSpec(memory_space=pltpu.VMEM)
    return pl.pallas_call(
        functools.partial(kernel, layers, nx, nz, heads, tokens),
        out_shape=jax.ShapeDtypeStruct((1, 1, tokens, width), bf16),
        in_specs=[any_space, any_space] + [in_vmem] * 4 + [pl.BlockSpec(memory_space=pltpu.SMEM), in_vmem],
        out_specs=any_space,
        scratch_shapes=[
            pltpu.VMEM((2, half, width), bf16),
            pltpu.VMEM((half, width), bf16),
            pltpu.VMEM((layers, width, cols), bf16),
            pltpu.VMEM((layers, 8, width), f32),
            pltpu.VMEM((heads, half, HEAD), bf16),
            pltpu.VMEM((2, heads, 2, half, 2 * HEAD), bf16),
            pltpu.VMEM((2, heads, 2, 2, half, 2 * HEAD), bf16),
            pltpu.VMEM((heads, half, 2 * HEAD), f32),
            pltpu.VMEM((3, SLOTS, 1, tokens), f32),
            dma((3,)), dma((3,)), dma((3,)), dma((3,)), dma((3,)),
            dma((pairs, 8)), dma((pairs, 8)), dma((3,)), dma((3,)),
            dma((pairs, 2, 2)), dma((pairs, 2, 2)), dma((pairs, 2)), dma((pairs, 2)),
            dma((pairs, 4)), dma((pairs, 4)), dma((pairs,)), dma((pairs,)),
            dma((2, heads, 5)), dma((2, heads, 5)), dma((2, heads, 3)), dma((2, heads, 3)),
            dma((1,)), dma((1,)), dma((1,)),
        ],
        compiler_params=pltpu.CompilerParams(
            collective_id=0, has_side_effects=True, vmem_limit_bytes=58 * 1024 * 1024
        ),
    )(latent, w_qkv, mod_shift, mod_scale, attn_gate, qk_gain, slot_tile, window_tiles.T)


def solution(mesh, nx=NX):
    return jax.shard_map(
        functools.partial(on_device, nx),
        mesh=mesh,
        in_specs=(
            P(None, "tile", None),
            P("section", "tile", None),
            P("section", None),
            P("section", None),
            P("section", None),
            P("section", None),
            P(),
            P(),
        ),
        out_specs=P("section", None, "tile", None),
        check_vma=False,
    )
```

```python
import functools
import math

import jax
import jax.numpy as jnp
from jax import lax
from jax.experimental import pallas as pl
from jax.experimental.pallas import tpu as pltpu
from jax.sharding import PartitionSpec as P

MESH = pl.DeviceIdType.MESH
HEAD = 128
SLOTS = 3
NY = 4
NX = 4
EPS = 1e-06
NEG = -1e30


def kernel(
    layers, nx, nz, heads, tokens, lat, w_part, shift_row, scale_row, gate_row, gain_row, slot_ids, windows, out,
    hbuf, mod, wbuf, parbuf, qbuf, kvo, kvn, acc, bias,
    loc_sem, a2a_s, a2a_r, par_s, par_r, z_s, z_r, x0_s, x0_r, x_s, x_r, xf_s, xf_r, c_s, c_r, cp_s, cp_r,
    kv_s, kv_r, g_s, g_r, o_s, o_r, o_l,
):
    width = NY * heads * HEAD
    half = tokens // 2
    chunk = half // SLOTS
    shard = w_part.shape[1]
    group = heads * HEAD
    n_tile = nx * nz
    section = lax.axis_index("section")
    t = lax.axis_index("tile")
    y, c = section // 2, section % 2
    x, z = t // nz, t % nz
    sib = (2 * y + 1 - c, t)
    t_next = (section, (t + 1) % n_tile)
    t_prev = (section, (t + n_tile - 1) % n_tile)
    x_next = (section, ((x + 1) % nx) * nz + z)
    x_prev = (section, ((x + nx - 1) % nx) * nz + z)

    def y_peer(d):
        return (2 * ((y + d) % NY) + c, t)

    z_order = []
    for d in range(1, nz // 2 + 1):
        z_order += [d] if 2 * d == nz else [d, nz - d]

    def z_peer(d):
        return (section, x * nz + (z + d) % nz)

    def remote(src, dst, send, recv, device):
        return pltpu.make_async_remote_copy(
            src_ref=src, dst_ref=dst, send_sem=send, recv_sem=recv, device_id=device, device_id_type=MESH
        )

    partners = [y_peer(1), y_peer(2), y_peer(3), sib, t_next, t_prev]
    partners += [z_peer(d) for d in z_order]
    if nx > 1:
        partners += [x_next, x_prev, (section, ((x + 2) % nx) * nz + z)]
    load_h = pltpu.make_async_copy(lat.at[0, pl.ds(pl.multiple_of(half * c, 16), half)], hbuf.at[0], loc_sem.at[0])
    load_h.start()
    own_rows = pl.ds(pl.multiple_of(shard * t, 16), shard)

    def w_slices(place):
        for i in range(3):
            start = pl.multiple_of(i * width + place * group, HEAD)
            yield w_part.at[0, :, pl.ds(start, group)], wbuf.at[section, own_rows, i * group : (i + 1) * group]

    own_shard = wbuf.at[section, own_rows]
    for src, dst in w_slices(y):
        pltpu.make_async_copy(src, dst, loc_sem.at[1]).start()
    parbuf[section] = jnp.zeros(parbuf.shape[1:], jnp.float32)
    for i, row in enumerate((shift_row, scale_row, gate_row)):
        parbuf[section, i : i + 1, :] = row[...]
    parbuf[section, 3:4, 0:HEAD] = gain_row[...]
    barrier = pltpu.get_barrier_semaphore()
    for device in partners:
        pl.semaphore_signal(barrier, inc=1, device_id=device, device_id_type=MESH)
    pl.semaphore_wait(barrier, len(partners))

    def a2a_start():
        for d in (1, 3, 2):
            for src, dst in w_slices((y + d) % NY):
                remote(src, dst, a2a_s.at[d - 1], a2a_r.at[d - 1], y_peer(d)).start()
            remote(parbuf.at[section], parbuf.at[section], par_s.at[d - 1], par_r.at[d - 1], y_peer(d)).start()

    def a2a_whole(d):
        return (
            remote(own_shard, own_shard, a2a_s.at[d - 1], a2a_r.at[d - 1], sib),
            remote(parbuf.at[section], parbuf.at[section], par_s.at[d - 1], par_r.at[d - 1], sib),
        )

    @pl.when(y == 0)
    def _():
        a2a_start()

    @pl.when(y != 0)
    def _():
        for copy in a2a_whole(y):
            copy.wait_recv()
        a2a_start()

    pltpu.make_async_copy(own_shard, own_shard, loc_sem.at[1]).wait()

    def a2a_finish():
        for d in (1, 2, 3):
            for copy in a2a_whole(d):
                copy.wait_send()

            @pl.when(d != y)
            def _():
                for copy in a2a_whole(d):
                    copy.wait_recv()

    def rows_of(xx, zz):
        return pl.ds(pl.multiple_of((xx * nz + zz) * shard, 16), shard)

    def z_copy(layer, d, back=False):
        k = layer // 2
        ref = wbuf.at[layer, rows_of(x, (z + nz - d) % nz if back else z)]
        return remote(ref, ref, z_s.at[k, d - 1], z_r.at[k, d - 1], z_peer(d))

    def z_start(layer, order=None):
        for d in z_order if order is None else order:
            z_copy(layer, d).start()

    def z_finish(layer):
        for d in z_order:
            z_copy(layer, d, True).wait_recv()
        for d in z_order:
            z_copy(layer, d).wait_send()

    block = nz * shard

    def x_rows(place, piece=None):
        if piece is None:
            return pl.ds(pl.multiple_of(place * block, 16), block)
        return pl.ds(pl.multiple_of(place * block + piece * (block // 2), 16), block // 2)

    def x_copy(layer, way, order):
        ref = wbuf.at[layer, x_rows(x, order if way == 0 else 1 - order)]
        k = layer // 2
        return remote(ref, ref, x_s.at[k, way, order], x_r.at[k, way, order], x_next if way == 0 else x_prev)

    def x_forward(layer, part, way):
        place = (x + nx - 1) % nx if way == 0 else (x + 1) % nx
        ref = wbuf.at[layer, x_rows(place, part)]
        k = layer // 2
        return remote(ref, ref, xf_s.at[k, part], xf_r.at[k, part], x_next if way == 0 else x_prev)

    def x_forward_early(layer):
        for way in range(2 if nx > 1 else 0):
            x_copy(layer, way, 0).wait_recv()

            @pl.when(z != (0 if way == 0 else nz - 1))
            def _():
                x_forward(layer, way, way).start()

    def x_forward_late(layer):
        for way in range(2 if nx > 1 else 0):

            @pl.when(z == (nz - 1 if way == 0 else 0))
            def _():
                x_copy(layer, way, 1).wait_recv()
                x_forward(layer, 1 - way, way).start()

    def core_copy(layer, d):
        k = layer // 2
        ref = wbuf.at[layer, x_rows((x + d) % nx)]
        return remote(ref, ref, c_s.at[k, d], c_r.at[k, d], sib)

    def core_par(layer):
        k = layer // 2
        return remote(parbuf.at[layer], parbuf.at[layer], cp_s.at[k], cp_r.at[k], sib)

    def x_event(layer):
        if nx > 1:
            for order in range(2):
                for way in range(2):
                    x_copy(layer, way, order).start()

    def core_first(layer):
        core_copy(layer, 0).start()
        core_par(layer).start()

    def core_second(layer):
        if nx > 1:
            for way in range(2):

                @pl.when(z != (nz - 1 if way == 0 else 0))
                def _():
                    x_copy(layer, way, 1).wait_recv()

                core_copy(layer, nx - 1 if way == 0 else 1).start()

    def core_last(layer):
        if nx > 1:
            for part in range(2):
                x_forward(layer, part, 0).wait_recv()
            core_copy(layer, 2).start()
            for part in range(2):
                x_copy(layer, 0, part).wait_send()
                x_copy(layer, 1, part).wait_send()
            for part in range(2):
                x_forward(layer, part, 0).wait_send()

    def x_direct(zz):
        ref = wbuf.at[0, rows_of(x, zz)]
        for d in (1, 3, 2) if nx == 4 else ():
            to = (section, ((x + d) % nx) * nz + z)
            remote(ref, ref, x0_s.at[d - 1], x0_r.at[d - 1], to).start()

    def x_direct_whole(d, back):
        ref = wbuf.at[0, x_rows((x + nx - d) % nx if back else x)]
        return remote(ref, ref, x0_s.at[d - 1], x0_r.at[d - 1], sib)

    @pl.when(c == 0)
    def _():
        z_start(0)
        x_direct(z)
        for d in z_order:
            z_copy(0, d, True).wait_recv()
            x_direct((z + nz - d) % nz)
        core_copy(0, 0).start()
        core_par(0).start()
        for d in z_order:
            z_copy(0, d).wait_send()
        a2a_finish()
        if nx > 1:
            for d in (1, 3, 2):
                x_direct_whole(d, True).wait_recv()
                core_copy(0, nx - d).start()
            for d in (1, 3, 2):
                x_direct_whole(d, False).wait_send()

    @pl.when(c == 1)
    def _():
        a2a_finish()
        core_copy(0, 0).wait_recv()
        core_par(0).wait_recv()
        z_start(1)
        for d in range(1, nx):
            core_copy(0, d).wait_recv()

    tile_len = tokens // SLOTS
    n_slots = n_tile * SLOTS
    lanes = lax.broadcasted_iota(jnp.int32, (1, tokens), 1)

    tile_lanes = lax.broadcasted_iota(jnp.int32, windows.shape, 1)

    def penalty(query_slot, frame, key_slot):
        place = (t + n_tile + frame) % n_tile
        key_id = slot_ids[place * SLOTS + key_slot]
        in_window = jnp.logical_and(tile_lanes == slot_ids[t * SLOTS + query_slot], windows[...] == key_id)
        listed = jnp.max(jnp.where(in_window, 1.0, 0.0), axis=(0, 1), keepdims=True)
        return jnp.where(listed > 0.0, 0.0, NEG)

    for i in range(SLOTS):
        query_slot = (half * c + chunk * i) // tile_len
        table = [[penalty(query_slot, frame, k) for k in range(SLOTS)] for frame in (-1, 0, 1)]

        def spread_over(tokens_at, pens):
            return jnp.where(tokens_at < tile_len, pens[0], jnp.where(tokens_at < 2 * tile_len, pens[1], pens[2]))

        bias[0, i] = spread_over(lanes, table[1])
        for side in range(2):
            low = spread_over(lanes + side * half, table[0])
            high = spread_over(lanes - half + side * half, table[2])
            bias[1 + side, i] = jnp.where(lanes < half, low, high)

    load_h.wait()

    ones = jnp.ones((tokens, HEAD), jnp.bfloat16)

    def dot(a, b):
        return jnp.dot(a, b, preferred_element_type=jnp.float32)

    def head_norm(numbers, gain):
        square_mean = jnp.mean(numbers * numbers, axis=-1, keepdims=True)
        return (numbers * lax.rsqrt(square_mean + EPS) * gain).astype(jnp.bfloat16)

    def one_block(j, keys, values, allowed):
        scores = lax.dot_general(
            qbuf[j], keys, (((1,), (1,)), ((), ())), preferred_element_type=jnp.float32
        )
        scores = scores.reshape(SLOTS, chunk, tokens) + allowed
        powers = jnp.exp2(scores).astype(jnp.bfloat16).reshape(half, tokens)
        return dot(powers, jnp.concatenate([values, ones], axis=1))

    def layer_step(layer, carry):
        p = layer % 2
        q = 1 - p

        def event(ahead, condition, do):
            ours = jnp.logical_and((layer + ahead) % 2 == c, layer + ahead < layers)
            if condition is not None:
                ours = jnp.logical_and(ours, condition)

            @pl.when(ours)
            def _():
                do(layer + ahead)

        def z_then_x(target):
            z_finish(target)
            x_event(target)

        def middle(target):
            x_forward_late(target)
            core_second(target)

        def first_end(target):
            x_forward_late(target)
            core_first(target)
            core_second(target)

        def at(place):
            if place == 0:
                event(1, layer == 0, z_then_x)
                event(1, layer > 1, x_forward_early)
                event(1, layer > 1, core_first)
            elif place == 1:
                event(1, layer > 1, middle)
            elif place == 2:
                event(1, layer <= 1, x_forward_early)
                event(2, layer > 0, z_then_x)
                event(2, layer == 0, z_start)
            elif place == 3:
                event(3, None, z_start)
            else:
                event(1, layer <= 1, first_end)
                event(1, None, core_last)
                event(2, layer == 0, z_then_x)

        @pl.when(jnp.logical_and(c != p, layer > 0))
        def _():
            core_par(layer).wait_recv()
            for d in range(nx):
                core_copy(layer, d).wait_recv()

        shifts = parbuf[layer, 0:1, :]
        scales = parbuf[layer, 1:2, :]
        gain = parbuf[layer, 3:4, 0:HEAD]
        for i in range(SLOTS):
            rows = pl.ds(i * chunk, chunk)
            numbers = hbuf[p, rows, :].astype(jnp.float32)
            average = jnp.mean(numbers, axis=-1, keepdims=True)
            centred = numbers - average
            spread = jnp.mean(centred * centred, axis=-1, keepdims=True)
            mod[rows, :] = (centred * lax.rsqrt(spread + EPS) * scales + shifts).astype(jnp.bfloat16)

        def kv_copy(j, kind):
            if kind == 0:
                ref = kvo.at[p, j, c]
                dst, device = ref, sib
            elif kind == 1:
                ref, dst, device = kvo.at[p, j, c], kvn.at[p, j, c, 0], t_next
            elif kind == 2:
                ref, dst, device = kvo.at[p, j, c], kvn.at[p, j, c, 1], t_prev
            else:
                ref = kvn.at[p, j, c, kind - 3]
                dst, device = ref, sib
            return remote(ref, dst, kv_s.at[p, j, kind], kv_r.at[p, j, kind], device)

        for j in range(heads):
            weights = jnp.concatenate(
                [wbuf[layer, :, i * group + HEAD * j : i * group + HEAD * (j + 1)] for i in (1, 2)], axis=1
            )
            projected = dot(mod[...], weights)
            kvo[p, j, c, :, 0:HEAD] = head_norm(projected[:, 0:HEAD], gain)
            kvo[p, j, c, :, HEAD : 2 * HEAD] = projected[:, HEAD:].astype(jnp.bfloat16)
            for kind in (1, 2, 0):
                kv_copy(j, kind).start()
        at(0)
        queries = dot(mod[...], wbuf[layer, :, 0:group])
        query_gain = gain * (math.log2(math.e) / math.sqrt(HEAD))
        for j in range(heads):
            qbuf[j] = head_norm(queries[:, HEAD * j : HEAD * (j + 1)], query_gain)

        @pl.when(section == layer - 1)
        def _():
            keep_own().wait()

        @pl.when(2 * y + 1 - c == layer - 1)
        def _():
            keep_other().wait_send()

        for j in range(heads):
            kv_copy(j, 0).wait_recv()
            block = kvo[p, j].reshape(tokens, 2 * HEAD)
            acc[j] = one_block(j, block[:, 0:HEAD], block[:, HEAD:], bias[0])
        at(1)

        def near(j, side):
            block = kvn[p, j, side].reshape(tokens, 2 * HEAD)
            return one_block(j, block[:, 0:HEAD], block[:, HEAD:], bias[1 + side])

        def pass_on(j):
            for kind in (1, 2):
                kv_copy(j, kind).wait_recv()
                kv_copy(j, kind + 2).start()
            acc[j] += near(j, c)

        def g_copy(j, d, back):
            place = (y + NY - d) % NY if back else y
            columns = pl.ds(pl.multiple_of((place * heads + j) * HEAD, HEAD), HEAD)
            ref = hbuf.at[q, :, columns]
            return remote(ref, ref, g_s.at[p, j, d - 1], g_r.at[p, j, d - 1], y_peer(d))

        def sends_to(d):
            return jnp.logical_or(layer < layers - 1, (y + d) % NY == NY - 1)

        def finish(j):
            for kind in (3, 4):
                kv_copy(j, kind).wait_recv()
            total = acc[j] + near(j, 1 - c)
            columns = pl.ds(pl.multiple_of((y * heads + j) * HEAD, HEAD), HEAD)
            attended = total[:, 0:HEAD] / total[:, HEAD:]
            gates = parbuf[layer, 2:3, columns]
            numbers = hbuf[p, :, columns].astype(jnp.float32) + gates * attended
            hbuf[q, :, columns] = numbers.astype(jnp.bfloat16)
            for d in (1, 3, 2):

                @pl.when(sends_to(d))
                def _():
                    g_copy(j, d, False).start()

        for j in range(heads):
            if j == heads - 1:
                at(3)
            pass_on(j)
            finish(j)
            if j == 0:
                at(2)
        at(4)
        for j in range(heads):
            for kind in range(5):
                kv_copy(j, kind).wait_send()
        for d in (1, 3, 2):

            @pl.when(sends_to(d))
            def _():
                for j in range(heads):
                    g_copy(j, d, False).wait_send()

        @pl.when(sends_to(0))
        def _():
            for j in range(heads):
                for d in (1, 3, 2):
                    g_copy(j, d, True).wait_recv()

        @pl.when(c == p)
        def _():
            core_par(layer).wait_send()
            for d in range(nx):
                core_copy(layer, d).wait_send()

        @pl.when(section == layer)
        def _():
            keep_own().start()

        @pl.when(2 * y + 1 - c == layer)
        def _():
            keep_other().start()

        return carry

    def out_rows(place):
        return out.at[0, 0, pl.ds(pl.multiple_of(half * place, 16), half)]

    def keep_own():
        return pltpu.make_async_copy(hbuf.at[1 - c], out_rows(c), o_l.at[0])

    def keep_other():
        return remote(hbuf.at[c], out_rows(c), o_s.at[0], o_r.at[0], sib)

    lax.fori_loop(0, layers, layer_step, 0)

    @pl.when(section == layers - 1)
    def _():
        keep_own().wait()

    @pl.when(2 * y + 1 - c == layers - 1)
    def _():
        keep_other().wait_send()

    remote(hbuf.at[c], out_rows(1 - c), o_s.at[0], o_r.at[0], sib).wait_recv()


def on_device(nx, latent, w_qkv, mod_shift, mod_scale, attn_gate, qk_gain, slot_tile, window_tiles):
    layers = lax.axis_size("section")
    n_tile = lax.axis_size("tile")
    nz = n_tile // nx
    _, tokens, width = latent.shape
    heads = width // HEAD // NY
    shard = w_qkv.shape[1]
    half = tokens // 2
    cols = 3 * heads * HEAD
    pairs = layers // 2
    bf16, f32 = jnp.bfloat16, jnp.float32
    dma = pltpu.SemaphoreType.DMA
    any_space = pl.BlockSpec(memory_space=pl.ANY)
    in_vmem = pl.BlockSpec(memory_space=pltpu.VMEM)
    return pl.pallas_call(
        functools.partial(kernel, layers, nx, nz, heads, tokens),
        out_shape=jax.ShapeDtypeStruct((1, 1, tokens, width), bf16),
        in_specs=[any_space, any_space] + [in_vmem] * 4 + [pl.BlockSpec(memory_space=pltpu.SMEM), in_vmem],
        out_specs=any_space,
        scratch_shapes=[
            pltpu.VMEM((2, half, width), bf16),
            pltpu.VMEM((half, width), bf16),
            pltpu.VMEM((layers, width, cols), bf16),
            pltpu.VMEM((layers, 8, width), f32),
            pltpu.VMEM((heads, half, HEAD), bf16),
            pltpu.VMEM((2, heads, 2, half, 2 * HEAD), bf16),
            pltpu.VMEM((2, heads, 2, 2, half, 2 * HEAD), bf16),
            pltpu.VMEM((heads, half, 2 * HEAD), f32),
            pltpu.VMEM((3, SLOTS, 1, tokens), f32),
            dma((3,)), dma((3,)), dma((3,)), dma((3,)), dma((3,)),
            dma((pairs, 8)), dma((pairs, 8)), dma((3,)), dma((3,)),
            dma((pairs, 2, 2)), dma((pairs, 2, 2)), dma((pairs, 2)), dma((pairs, 2)),
            dma((pairs, 4)), dma((pairs, 4)), dma((pairs,)), dma((pairs,)),
            dma((2, heads, 5)), dma((2, heads, 5)), dma((2, heads, 3)), dma((2, heads, 3)),
            dma((1,)), dma((1,)), dma((1,)),
        ],
        compiler_params=pltpu.CompilerParams(
            collective_id=0, has_side_effects=True, vmem_limit_bytes=58 * 1024 * 1024
        ),
    )(latent, w_qkv, mod_shift, mod_scale, attn_gate, qk_gain, slot_tile, window_tiles.T)


def solution(mesh, nx=NX):
    return jax.shard_map(
        functools.partial(on_device, nx),
        mesh=mesh,
        in_specs=(
            P(None, "tile", None),
            P("section", "tile", None),
            P("section", None),
            P("section", None),
            P("section", None),
            P("section", None),
            P(),
            P(),
        ),
        out_specs=P("section", None, "tile", None),
        check_vma=False,
    )
```

```python
import functools
import math

import jax
import jax.numpy as jnp
from jax import lax
from jax.experimental import pallas as pl
from jax.experimental.pallas import tpu as pltpu
from jax.sharding import PartitionSpec as P

MESH = pl.DeviceIdType.MESH
HEAD = 128
SLOTS = 3
NY = 4
NX = 4
EPS = 1e-06
NEG = -1e30


def kernel(
    layers, nx, nz, heads, tokens, lat, w_part, shift_row, scale_row, gate_row, gain_row, slot_ids, windows, out,
    hbuf, mod, wbuf, parbuf, qbuf, kvo, kvn, acc, bias,
    loc_sem, a2a_s, a2a_r, par_s, par_r, z_s, z_r, x0_s, x0_r, x_s, x_r, xf_s, xf_r, c_s, c_r, cp_s, cp_r,
    kv_s, kv_r, g_s, g_r, o_s, o_r, o_l,
):
    width = NY * heads * HEAD
    half = tokens // 2
    chunk = half // SLOTS
    shard = w_part.shape[1]
    group = heads * HEAD
    n_tile = nx * nz
    section = lax.axis_index("section")
    t = lax.axis_index("tile")
    y, c = section // 2, section % 2
    x, z = t // nz, t % nz
    sib = (2 * y + 1 - c, t)
    t_next = (section, (t + 1) % n_tile)
    t_prev = (section, (t + n_tile - 1) % n_tile)
    x_next = (section, ((x + 1) % nx) * nz + z)
    x_prev = (section, ((x + nx - 1) % nx) * nz + z)

    def y_peer(d):
        return (2 * ((y + d) % NY) + c, t)

    z_order = []
    for d in range(1, nz // 2 + 1):
        z_order += [d] if 2 * d == nz else [d, nz - d]

    def z_peer(d):
        return (section, x * nz + (z + d) % nz)

    def remote(src, dst, send, recv, device):
        return pltpu.make_async_remote_copy(
            src_ref=src, dst_ref=dst, send_sem=send, recv_sem=recv, device_id=device, device_id_type=MESH
        )

    partners = [y_peer(1), y_peer(2), y_peer(3), sib, t_next, t_prev]
    partners += [z_peer(d) for d in z_order]
    if nx > 1:
        partners += [x_next, x_prev, (section, ((x + 2) % nx) * nz + z)]
    load_h = pltpu.make_async_copy(lat.at[0, pl.ds(pl.multiple_of(half * c, 16), half)], hbuf.at[0], loc_sem.at[0])
    load_h.start()
    own_rows = pl.ds(pl.multiple_of(shard * t, 16), shard)

    def w_slices(place):
        for i in range(3):
            start = pl.multiple_of(i * width + place * group, HEAD)
            yield w_part.at[0, :, pl.ds(start, group)], wbuf.at[section, own_rows, i * group : (i + 1) * group]

    own_shard = wbuf.at[section, own_rows]
    for src, dst in w_slices(y):
        pltpu.make_async_copy(src, dst, loc_sem.at[1]).start()
    parbuf[section] = jnp.zeros(parbuf.shape[1:], jnp.float32)
    for i, row in enumerate((shift_row, scale_row, gate_row)):
        parbuf[section, i : i + 1, :] = row[...]
    parbuf[section, 3:4, 0:HEAD] = gain_row[...]
    barrier = pltpu.get_barrier_semaphore()
    for device in partners:
        pl.semaphore_signal(barrier, inc=1, device_id=device, device_id_type=MESH)
    pl.semaphore_wait(barrier, len(partners))

    def a2a_start():
        for d in (1, 3, 2):
            for src, dst in w_slices((y + d) % NY):
                remote(src, dst, a2a_s.at[d - 1], a2a_r.at[d - 1], y_peer(d)).start()
            remote(parbuf.at[section], parbuf.at[section], par_s.at[d - 1], par_r.at[d - 1], y_peer(d)).start()

    def a2a_whole(d):
        return (
            remote(own_shard, own_shard, a2a_s.at[d - 1], a2a_r.at[d - 1], sib),
            remote(parbuf.at[section], parbuf.at[section], par_s.at[d - 1], par_r.at[d - 1], sib),
        )

    @pl.when(y == 0)
    def _():
        a2a_start()

    @pl.when(y != 0)
    def _():
        for copy in a2a_whole(y):
            copy.wait_recv()
        a2a_start()

    pltpu.make_async_copy(own_shard, own_shard, loc_sem.at[1]).wait()

    def a2a_finish():
        for d in (1, 2, 3):
            for copy in a2a_whole(d):
                copy.wait_send()

            @pl.when(d != y)
            def _():
                for copy in a2a_whole(d):
                    copy.wait_recv()

    def rows_of(xx, zz):
        return pl.ds(pl.multiple_of((xx * nz + zz) * shard, 16), shard)

    def z_copy(layer, d, back=False):
        k = layer // 2
        ref = wbuf.at[layer, rows_of(x, (z + nz - d) % nz if back else z)]
        return remote(ref, ref, z_s.at[k, d - 1], z_r.at[k, d - 1], z_peer(d))

    def z_start(layer, order=None):
        for d in z_order if order is None else order:
            z_copy(layer, d).start()

    def z_finish(layer):
        for d in z_order:
            z_copy(layer, d, True).wait_recv()
        for d in z_order:
            z_copy(layer, d).wait_send()

    block = nz * shard

    def x_rows(place, piece=None):
        if piece is None:
            return pl.ds(pl.multiple_of(place * block, 16), block)
        return pl.ds(pl.multiple_of(place * block + piece * (block // 2), 16), block // 2)

    def x_copy(layer, way, order):
        ref = wbuf.at[layer, x_rows(x, order if way == 0 else 1 - order)]
        k = layer // 2
        return remote(ref, ref, x_s.at[k, way, order], x_r.at[k, way, order], x_next if way == 0 else x_prev)

    def x_forward(layer, part, way):
        place = (x + nx - 1) % nx if way == 0 else (x + 1) % nx
        ref = wbuf.at[layer, x_rows(place, part)]
        k = layer // 2
        return remote(ref, ref, xf_s.at[k, part], xf_r.at[k, part], x_next if way == 0 else x_prev)

    def x_forward_early(layer):
        for way in range(2 if nx > 1 else 0):
            x_copy(layer, way, 0).wait_recv()

            @pl.when(z != (0 if way == 0 else nz - 1))
            def _():
                x_forward(layer, way, way).start()

    def x_forward_late(layer):
        for way in range(2 if nx > 1 else 0):

            @pl.when(z == (nz - 1 if way == 0 else 0))
            def _():
                x_copy(layer, way, 1).wait_recv()
                x_forward(layer, 1 - way, way).start()

    def core_copy(layer, d):
        k = layer // 2
        ref = wbuf.at[layer, x_rows((x + d) % nx)]
        return remote(ref, ref, c_s.at[k, d], c_r.at[k, d], sib)

    def core_par(layer):
        k = layer // 2
        return remote(parbuf.at[layer], parbuf.at[layer], cp_s.at[k], cp_r.at[k], sib)

    def x_event(layer):
        if nx > 1:
            for order in range(2):
                for way in range(2):
                    x_copy(layer, way, order).start()

    def core_first(layer):
        core_copy(layer, 0).start()
        core_par(layer).start()

    def core_second(layer):
        if nx > 1:
            for way in range(2):

                @pl.when(z != (nz - 1 if way == 0 else 0))
                def _():
                    x_copy(layer, way, 1).wait_recv()

                core_copy(layer, nx - 1 if way == 0 else 1).start()

    def core_last(layer):
        if nx > 1:
            for part in range(2):
                x_forward(layer, part, 0).wait_recv()
            core_copy(layer, 2).start()
            for part in range(2):
                x_copy(layer, 0, part).wait_send()
                x_copy(layer, 1, part).wait_send()
            for part in range(2):
                x_forward(layer, part, 0).wait_send()

    def x_direct(zz):
        ref = wbuf.at[0, rows_of(x, zz)]
        for d in (1, 3, 2) if nx == 4 else ():
            to = (section, ((x + d) % nx) * nz + z)
            remote(ref, ref, x0_s.at[d - 1], x0_r.at[d - 1], to).start()

    def x_direct_whole(d, back):
        ref = wbuf.at[0, x_rows((x + nx - d) % nx if back else x)]
        return remote(ref, ref, x0_s.at[d - 1], x0_r.at[d - 1], sib)

    @pl.when(c == 0)
    def _():
        z_start(0)
        x_direct(z)
        for d in z_order:
            z_copy(0, d, True).wait_recv()
            x_direct((z + nz - d) % nz)
        core_copy(0, 0).start()
        core_par(0).start()
        for d in z_order:
            z_copy(0, d).wait_send()
        a2a_finish()

    tile_len = tokens // SLOTS
    n_slots = n_tile * SLOTS
    lanes = lax.broadcasted_iota(jnp.int32, (1, tokens), 1)

    tile_lanes = lax.broadcasted_iota(jnp.int32, windows.shape, 1)

    def penalty(query_slot, frame, key_slot):
        place = (t + n_tile + frame) % n_tile
        key_id = slot_ids[place * SLOTS + key_slot]
        in_window = jnp.logical_and(tile_lanes == slot_ids[t * SLOTS + query_slot], windows[...] == key_id)
        listed = jnp.max(jnp.where(in_window, 1.0, 0.0), axis=(0, 1), keepdims=True)
        return jnp.where(listed > 0.0, 0.0, NEG)

    for i in range(SLOTS):
        query_slot = (half * c + chunk * i) // tile_len
        table = [[penalty(query_slot, frame, k) for k in range(SLOTS)] for frame in (-1, 0, 1)]

        def spread_over(tokens_at, pens):
            return jnp.where(tokens_at < tile_len, pens[0], jnp.where(tokens_at < 2 * tile_len, pens[1], pens[2]))

        bias[0, i] = spread_over(lanes, table[1])
        for side in range(2):
            low = spread_over(lanes + side * half, table[0])
            high = spread_over(lanes - half + side * half, table[2])
            bias[1 + side, i] = jnp.where(lanes < half, low, high)

    @pl.when(c == 0)
    def _():
        if nx > 1:
            for d in (1, 3, 2):
                x_direct_whole(d, True).wait_recv()
                core_copy(0, nx - d).start()
            for d in (1, 3, 2):
                x_direct_whole(d, False).wait_send()

    @pl.when(c == 1)
    def _():
        a2a_finish()
        core_copy(0, 0).wait_recv()
        core_par(0).wait_recv()
        z_start(1)
        for d in range(1, nx):
            core_copy(0, d).wait_recv()

    load_h.wait()

    ones = jnp.ones((tokens, HEAD), jnp.bfloat16)

    def dot(a, b):
        return jnp.dot(a, b, preferred_element_type=jnp.float32)

    def head_norm(numbers, gain):
        square_mean = jnp.mean(numbers * numbers, axis=-1, keepdims=True)
        return (numbers * lax.rsqrt(square_mean + EPS) * gain).astype(jnp.bfloat16)

    def one_block(j, keys, values, allowed):
        scores = lax.dot_general(
            qbuf[j], keys, (((1,), (1,)), ((), ())), preferred_element_type=jnp.float32
        )
        scores = scores.reshape(SLOTS, chunk, tokens) + allowed
        powers = jnp.exp2(scores).astype(jnp.bfloat16).reshape(half, tokens)
        return dot(powers, jnp.concatenate([values, ones], axis=1))

    def layer_step(layer, carry):
        p = layer % 2
        q = 1 - p

        def event(ahead, condition, do):
            ours = jnp.logical_and((layer + ahead) % 2 == c, layer + ahead < layers)
            if condition is not None:
                ours = jnp.logical_and(ours, condition)

            @pl.when(ours)
            def _():
                do(layer + ahead)

        def z_then_x(target):
            z_finish(target)
            x_event(target)

        def middle(target):
            x_forward_late(target)
            core_second(target)

        def first_end(target):
            x_forward_late(target)
            core_first(target)
            core_second(target)

        def at(place):
            if place == 0:
                event(1, layer == 0, z_then_x)
                event(1, layer > 1, x_forward_early)
                event(1, layer > 1, core_first)
            elif place == 1:
                event(1, layer > 1, middle)
            elif place == 2:
                event(1, layer <= 1, x_forward_early)
                event(2, layer > 0, z_then_x)
                event(2, layer == 0, z_start)
            elif place == 3:
                event(3, None, z_start)
            else:
                event(1, layer <= 1, first_end)
                event(1, None, core_last)
                event(2, layer == 0, z_then_x)

        @pl.when(jnp.logical_and(c != p, layer > 0))
        def _():
            core_par(layer).wait_recv()
            for d in range(nx):
                core_copy(layer, d).wait_recv()

        shifts = parbuf[layer, 0:1, :]
        scales = parbuf[layer, 1:2, :]
        gain = parbuf[layer, 3:4, 0:HEAD]
        for i in range(SLOTS):
            rows = pl.ds(i * chunk, chunk)
            numbers = hbuf[p, rows, :].astype(jnp.float32)
            average = jnp.mean(numbers, axis=-1, keepdims=True)
            centred = numbers - average
            spread = jnp.mean(centred * centred, axis=-1, keepdims=True)
            mod[rows, :] = (centred * lax.rsqrt(spread + EPS) * scales + shifts).astype(jnp.bfloat16)

        def kv_copy(j, kind):
            if kind == 0:
                ref = kvo.at[p, j, c]
                dst, device = ref, sib
            elif kind == 1:
                ref, dst, device = kvo.at[p, j, c], kvn.at[p, j, c, 0], t_next
            elif kind == 2:
                ref, dst, device = kvo.at[p, j, c], kvn.at[p, j, c, 1], t_prev
            else:
                ref = kvn.at[p, j, c, kind - 3]
                dst, device = ref, sib
            return remote(ref, dst, kv_s.at[p, j, kind], kv_r.at[p, j, kind], device)

        for j in range(heads):
            weights = jnp.concatenate(
                [wbuf[layer, :, i * group + HEAD * j : i * group + HEAD * (j + 1)] for i in (1, 2)], axis=1
            )
            projected = dot(mod[...], weights)
            kvo[p, j, c, :, 0:HEAD] = head_norm(projected[:, 0:HEAD], gain)
            kvo[p, j, c, :, HEAD : 2 * HEAD] = projected[:, HEAD:].astype(jnp.bfloat16)
            for kind in (1, 2, 0):
                kv_copy(j, kind).start()
        at(0)
        queries = dot(mod[...], wbuf[layer, :, 0:group])
        query_gain = gain * (math.log2(math.e) / math.sqrt(HEAD))
        for j in range(heads):
            qbuf[j] = head_norm(queries[:, HEAD * j : HEAD * (j + 1)], query_gain)

        @pl.when(section == layer - 1)
        def _():
            keep_own().wait()

        @pl.when(2 * y + 1 - c == layer - 1)
        def _():
            keep_other().wait_send()

        for j in range(heads):
            kv_copy(j, 0).wait_recv()
            block = kvo[p, j].reshape(tokens, 2 * HEAD)
            acc[j] = one_block(j, block[:, 0:HEAD], block[:, HEAD:], bias[0])
        at(1)

        def near(j, side):
            block = kvn[p, j, side].reshape(tokens, 2 * HEAD)
            return one_block(j, block[:, 0:HEAD], block[:, HEAD:], bias[1 + side])

        def pass_on(j):
            for kind in (1, 2):
                kv_copy(j, kind).wait_recv()
                kv_copy(j, kind + 2).start()
            acc[j] += near(j, c)

        def g_copy(j, d, back):
            place = (y + NY - d) % NY if back else y
            columns = pl.ds(pl.multiple_of((place * heads + j) * HEAD, HEAD), HEAD)
            ref = hbuf.at[q, :, columns]
            return remote(ref, ref, g_s.at[p, j, d - 1], g_r.at[p, j, d - 1], y_peer(d))

        def sends_to(d):
            return jnp.logical_or(layer < layers - 1, (y + d) % NY == NY - 1)

        def finish(j):
            for kind in (3, 4):
                kv_copy(j, kind).wait_recv()
            total = acc[j] + near(j, 1 - c)
            columns = pl.ds(pl.multiple_of((y * heads + j) * HEAD, HEAD), HEAD)
            attended = total[:, 0:HEAD] / total[:, HEAD:]
            gates = parbuf[layer, 2:3, columns]
            numbers = hbuf[p, :, columns].astype(jnp.float32) + gates * attended
            hbuf[q, :, columns] = numbers.astype(jnp.bfloat16)
            for d in (1, 3, 2):

                @pl.when(sends_to(d))
                def _():
                    g_copy(j, d, False).start()

        for j in range(heads):
            if j == heads - 1:
                at(3)
            pass_on(j)
            finish(j)
            if j == 0:
                at(2)
        at(4)
        for j in range(heads):
            for kind in range(5):
                kv_copy(j, kind).wait_send()
        for d in (1, 3, 2):

            @pl.when(sends_to(d))
            def _():
                for j in range(heads):
                    g_copy(j, d, False).wait_send()

        @pl.when(sends_to(0))
        def _():
            for j in range(heads):
                for d in (1, 3, 2):
                    g_copy(j, d, True).wait_recv()

        @pl.when(c == p)
        def _():
            core_par(layer).wait_send()
            for d in range(nx):
                core_copy(layer, d).wait_send()

        @pl.when(section == layer)
        def _():
            keep_own().start()

        @pl.when(2 * y + 1 - c == layer)
        def _():
            keep_other().start()

        return carry

    def out_rows(place):
        return out.at[0, 0, pl.ds(pl.multiple_of(half * place, 16), half)]

    def keep_own():
        return pltpu.make_async_copy(hbuf.at[1 - c], out_rows(c), o_l.at[0])

    def keep_other():
        return remote(hbuf.at[c], out_rows(c), o_s.at[0], o_r.at[0], sib)

    lax.fori_loop(0, layers, layer_step, 0)

    @pl.when(section == layers - 1)
    def _():
        keep_own().wait()

    @pl.when(2 * y + 1 - c == layers - 1)
    def _():
        keep_other().wait_send()

    remote(hbuf.at[c], out_rows(1 - c), o_s.at[0], o_r.at[0], sib).wait_recv()


def on_device(nx, latent, w_qkv, mod_shift, mod_scale, attn_gate, qk_gain, slot_tile, window_tiles):
    layers = lax.axis_size("section")
    n_tile = lax.axis_size("tile")
    nz = n_tile // nx
    _, tokens, width = latent.shape
    heads = width // HEAD // NY
    shard = w_qkv.shape[1]
    half = tokens // 2
    cols = 3 * heads * HEAD
    pairs = layers // 2
    bf16, f32 = jnp.bfloat16, jnp.float32
    dma = pltpu.SemaphoreType.DMA
    any_space = pl.BlockSpec(memory_space=pl.ANY)
    in_vmem = pl.BlockSpec(memory_space=pltpu.VMEM)
    return pl.pallas_call(
        functools.partial(kernel, layers, nx, nz, heads, tokens),
        out_shape=jax.ShapeDtypeStruct((1, 1, tokens, width), bf16),
        in_specs=[any_space, any_space] + [in_vmem] * 4 + [pl.BlockSpec(memory_space=pltpu.SMEM), in_vmem],
        out_specs=any_space,
        scratch_shapes=[
            pltpu.VMEM((2, half, width), bf16),
            pltpu.VMEM((half, width), bf16),
            pltpu.VMEM((layers, width, cols), bf16),
            pltpu.VMEM((layers, 8, width), f32),
            pltpu.VMEM((heads, half, HEAD), bf16),
            pltpu.VMEM((2, heads, 2, half, 2 * HEAD), bf16),
            pltpu.VMEM((2, heads, 2, 2, half, 2 * HEAD), bf16),
            pltpu.VMEM((heads, half, 2 * HEAD), f32),
            pltpu.VMEM((3, SLOTS, 1, tokens), f32),
            dma((3,)), dma((3,)), dma((3,)), dma((3,)), dma((3,)),
            dma((pairs, 8)), dma((pairs, 8)), dma((3,)), dma((3,)),
            dma((pairs, 2, 2)), dma((pairs, 2, 2)), dma((pairs, 2)), dma((pairs, 2)),
            dma((pairs, 4)), dma((pairs, 4)), dma((pairs,)), dma((pairs,)),
            dma((2, heads, 5)), dma((2, heads, 5)), dma((2, heads, 3)), dma((2, heads, 3)),
            dma((1,)), dma((1,)), dma((1,)),
        ],
        compiler_params=pltpu.CompilerParams(
            collective_id=0, has_side_effects=True, vmem_limit_bytes=58 * 1024 * 1024
        ),
    )(latent, w_qkv, mod_shift, mod_scale, attn_gate, qk_gain, slot_tile, window_tiles.T)


def solution(mesh, nx=NX):
    return jax.shard_map(
        functools.partial(on_device, nx),
        mesh=mesh,
        in_specs=(
            P(None, "tile", None),
            P("section", "tile", None),
            P("section", None),
            P("section", None),
            P("section", None),
            P("section", None),
            P(),
            P(),
        ),
        out_specs=P("section", None, "tile", None),
        check_vma=False,
    )
```
